128 devices in a mesh: span: 4 (over z), stream: 32 (over y, x, core).
Axes of the slice: x: 4, y: 4, z: 4, core: 2. Of those that a mesh axis runs over, the one named last changes fastest.
Arguments:
- conserved_vector: float32 [5, 16, 512, 512], P(None, 'span', 'stream'), may hold values from -1 to 4, as said below
- occupied_patches: int32 [128], P(('span', 'stream')), may hold values from 0 to 8, as said below
- reading_volume: int32 [128, 128, 8], P(('span', 'stream')), may hold values from 0 to 32767, as said below
- reading_surface: int32 [128, 128, 8], P(('span', 'stream')), may hold values from -1 to 1023, as said below
- reading_elevation: float32 [131072], P(('span', 'stream')), may hold values from 0.5 to 2
- airfoil_surface_kelvin: float32 [131072], P(('span', 'stream')), may hold values from 0.5 to 0.9
Outputs:
- new_field: float32 [5, 16, 512, 512], P(None, 'span', 'stream')
- wall_flux: float32 [2, 131072], P(None, ('span', 'stream'))
The draws below stay inside these ranges and needn't reach their ends.
Inputs may be any that keep to these rules, and one draw needn't show every extreme that they name: `conserved_vector`: density 0.8 to 1.2, streamwise velocity 0.25 to 0.55, radial and pitchwise velocities within 0.15 in magnitude, pressure 0.8 to 1.2, energy = pressure / 0.4 plus half density times speed squared. The live faces of a device are its first 128 * occupied_patches ones; some device is full in every draw. `reading_volume`: a local cell number of the source's block. `reading_surface`: -1 marks an empty slot; each live face of the receiver appears exactly once over all sources and slots, no other face appears; a full receiver fills all 8 slots from every source.
All inputs are finite; a program needn't handle non-finite values.
Results may differ from the reference program's by a relative error of at most 0.0001.
Values sent between devices are 32-bit elements; how exact they have to be, the bound alone decides.
No kernel may reach another device: no remote copies, remote signals or barrier semaphores. Data moves between devices by JAX's collectives and lax.ppermute only.
A program may use at most 64 MiB of HBM per device.

```python
import math
import jax
import jax.numpy as jnp
from jax import lax

CS = 4
CT = 16
NP = 512
FACES_DEV = 1024
TILE = 128
NPTS = 64
ITERS = 6
NS = 16
NT = 512
CAP = 8
TILES = 8
SURFACE_SLOTS = 131072
N_STREAM = 32
DEVICES = 128


def tile_counts(key):
    key = jax.random.fold_in(key, 11)
    first_key, second_key = jax.random.split(key)
    partial_load = jax.random.randint(first_key, (DEVICES,), 0, TILES // 2 + 1)
    ranking = jax.random.permutation(second_key, DEVICES)
    return jnp.where(ranking < max(1, DEVICES // 4), TILES, partial_load).astype(jnp.int32)


def draw_occupied_patches(key, part):
    return tile_counts(key)


def draw_reading_surface(key, part):
    tile_loads = tile_counts(key)
    key = jax.random.fold_in(key, 2)
    place_key, source_key = jax.random.split(key)
    positions = jax.vmap(lambda sub_key: jax.random.permutation(sub_key, FACES_DEV))(jax.random.split(place_key, DEVICES))
    sources = jax.vmap(lambda sub_key: jax.random.permutation(sub_key, DEVICES))(jax.random.split(source_key, DEVICES))
    sender = jnp.take_along_axis(sources, positions % DEVICES, axis=1)
    slot_pos = positions // DEVICES
    face_ids = jnp.arange(FACES_DEV, dtype=jnp.int32)[None]
    face_value = jnp.where(face_ids < TILE * tile_loads[:, None], face_ids, -1).astype(jnp.int32)
    owner_id = jnp.broadcast_to(jnp.arange(DEVICES, dtype=jnp.int32)[:, None], face_value.shape)
    face_list = jnp.full((DEVICES, DEVICES, CAP), -1, jnp.int32)
    return face_list.at[owner_id, sender, slot_pos].set(face_value)


def draw_reading_volume(key, part):
    key = jax.random.fold_in(key, 3)
    chosen = jax.random.randint(key, (DEVICES, DEVICES, CAP), 0, CS * CT * NP).astype(jnp.int32)
    return chosen.at[0, 0, 0].set(CS * CT * NP - 1)


def draw_conserved_vector(key, part):
    key = jax.random.fold_in(key, 4)
    sub_keys = jax.random.split(key, 5)
    grid_shape = (NS, NT, NP)
    uniforms = [jax.random.uniform(sub_key, grid_shape, jnp.float32) for sub_key in sub_keys]
    fluid_rho_value = 0.8 + 0.4 * uniforms[0]
    streamwise = 0.25 + 0.3 * uniforms[1]
    radial = 0.15 * (2.0 * uniforms[2] - 1.0)
    pitchwise = 0.15 * (2.0 * uniforms[3] - 1.0)
    pressure = 0.8 + 0.4 * uniforms[4]
    energy = pressure / 0.4 + 0.5 * fluid_rho_value * (streamwise * streamwise + radial * radial + pitchwise * pitchwise)
    return jnp.stack([fluid_rho_value, fluid_rho_value * radial, fluid_rho_value * streamwise, fluid_rho_value * pitchwise, energy])


def steps_of(own_key, shape, pieces, low, largest):
    gain = 1.0
    for dim, shards_of in pieces:
        steps = jax.random.uniform(jax.random.fold_in(jax.random.fold_in(own_key, 6), dim), (shards_of,), jnp.float32, low / len(pieces), largest / len(pieces))
        gain = gain * jnp.repeat(jnp.exp(steps), shape[dim] // shards_of).reshape((-1,) + (1,) * (len(shape) - 1 - dim))
    return gain


def setup_inputs(seed: int = 0) -> dict:
    arg_keys = jax.random.split(jax.random.key(seed), 7)
    conserved_vector = draw_conserved_vector(jax.random.fold_in(arg_keys[6], 71), 0)
    occupied_patches = draw_occupied_patches(jax.random.fold_in(arg_keys[6], 71), 0)
    reading_volume = draw_reading_volume(jax.random.fold_in(arg_keys[6], 71), 0)
    reading_surface = draw_reading_surface(jax.random.fold_in(arg_keys[6], 71), 0)
    reading_elevation = jnp.clip(jnp.exp(math.log(2.0) - 1.3862944 * jax.random.uniform(arg_keys[4], (SURFACE_SLOTS,), jnp.float32) ** steps_of(arg_keys[4], (SURFACE_SLOTS,), ((0, 128),), -0.2, 0.2)), 0.5, 2.0)
    airfoil_surface_kelvin = jnp.clip(0.5 + 0.39999998 * jax.random.uniform(arg_keys[5], (SURFACE_SLOTS,), jnp.float32) ** steps_of(arg_keys[5], (SURFACE_SLOTS,), ((0, 128),), -0.2, 0.2), 0.5, 0.9)
    return {"conserved_vector": conserved_vector, "occupied_patches": occupied_patches, "reading_volume": reading_volume, "reading_surface": reading_surface, "reading_elevation": reading_elevation, "airfoil_surface_kelvin": airfoil_surface_kelvin}


adiabatic_exponent = 1.4
time_step = 0.1
viscosity = 0.02
dynamic_internal_friction = 0.002
von_karman = 0.41
damping_plus = 17.0
diffusivity_quotient = 0.72
prandtl_turb = 0.9
isobaric_caloric_constant = 3.5
stretch = 3.0

def segment(array, offset, extent, axis_pos):
    return lax.slice_in_dim(array, offset, offset + extent, axis=axis_pos)

def primitive(fields):
    fluid_rho_value = fields[0]
    velocity = fields[1:4] / fluid_rho_value
    pressure = (adiabatic_exponent - 1.0) * (fields[4] - 0.5 * lax.optimization_barrier(jnp.sum(fields[1:4] * velocity, axis=0)))
    sound_speed = jnp.sqrt(adiabatic_exponent * pressure / fluid_rho_value)
    return (velocity, pressure, sound_speed)

def direction_terms(fields, normal_speed, pressure, sound_speed, normal, axis_pos):
    phys_flux = fields * normal_speed[None]
    phys_flux = phys_flux.at[1 + normal].add(pressure)
    phys_flux = phys_flux.at[4].add(pressure * normal_speed)
    wave_speed = jnp.abs(normal_speed) + sound_speed
    extent = fields.shape[axis_pos]
    difference = segment(fields, 1, extent - 1, axis_pos) - segment(fields, 0, extent - 1, axis_pos)
    max_speed = jnp.maximum(segment(wave_speed, 1, extent - 1, axis_pos - 1), segment(wave_speed, 0, extent - 1, axis_pos - 1))
    face_values = 0.5 * (segment(phys_flux, 1, extent - 1, axis_pos) + segment(phys_flux, 0, extent - 1, axis_pos)) - 0.5 * max_speed[None] * difference
    divergence = segment(face_values, 1, extent - 2, axis_pos) - segment(face_values, 0, extent - 2, axis_pos)
    curvature = segment(difference, 1, extent - 2, axis_pos) - segment(difference, 0, extent - 2, axis_pos)
    return (divergence, curvature)

def wrap_pitch(array):
    return jnp.concatenate([array[..., -1:], array, array[..., :1]], axis=-1)

def tendency(extended):
    velocity, pressure, sound_speed = primitive(extended)
    span_div, span_curv = direction_terms(extended[:, :, 1:-1], velocity[0, :, 1:-1], pressure[:, 1:-1], sound_speed[:, 1:-1], 0, 1)
    stream_div, stream_curv = direction_terms(extended[:, 1:-1], velocity[1, 1:-1], pressure[1:-1], sound_speed[1:-1], 1, 2)
    pitch_div, pitch_curv = direction_terms(wrap_pitch(extended[:, 1:-1, 1:-1]), wrap_pitch(velocity[2, 1:-1, 1:-1]), wrap_pitch(pressure[1:-1, 1:-1]), wrap_pitch(sound_speed[1:-1, 1:-1]), 2, 3)
    weights = jnp.array([0.0, 1.0, 1.0, 1.0, 1.0], jnp.float32)[:, None, None, None]
    return -(span_div + stream_div + pitch_div) + viscosity * weights * (span_curv + stream_curv + pitch_curv)

def full_tendency(conserved_vector):
    padded = jnp.pad(conserved_vector, ((0, 0), (1, 1), (1, 1), (0, 0)), mode='edge')

    def one_block(block_id):
        window = lax.dynamic_slice_in_dim(padded, block_id * CT, CT + 2, axis=2)
        return tendency(window)
    blocks = lax.map(one_block, jnp.arange(N_STREAM, dtype=jnp.int32))
    return jnp.moveaxis(blocks, 0, 2).reshape(5, NS, NT, NP)

def surface_closure(sensing_readings, sensing_elevation, airfoil_surface_kelvin):
    fluid_rho_value = sensing_readings[0]
    impulse_norm_power = lax.optimization_barrier(jnp.sum(sensing_readings[1:4] * sensing_readings[1:4], axis=0))
    speed = jnp.sqrt(impulse_norm_power) / fluid_rho_value
    fluid_kelvin = (adiabatic_exponent - 1.0) * (sensing_readings[4] - 0.5 * impulse_norm_power / fluid_rho_value) / fluid_rho_value
    levels = jnp.arange(NPTS, dtype=jnp.float32)[:, None] / (NPTS - 1)
    heights = sensing_elevation[None] * (jnp.exp(stretch * levels) - 1.0) / (math.exp(stretch) - 1.0)
    spacing = heights[1:] - heights[:-1]
    middle = 0.5 * (heights[1:] + heights[:-1])
    tangential_traction = dynamic_internal_friction * speed / sensing_elevation
    surface_enthalpy_rate = isobaric_caloric_constant * (dynamic_internal_friction / diffusivity_quotient) * (fluid_kelvin - airfoil_surface_kelvin) / sensing_elevation
    for iteration in range(ITERS):
        friction = jnp.sqrt(tangential_traction / fluid_rho_value)
        wall_units = middle * friction * fluid_rho_value / dynamic_internal_friction
        eddy_visc = fluid_rho_value * von_karman * middle * friction * (1.0 - jnp.exp(-wall_units / damping_plus)) ** 2
        increment = tangential_traction * spacing / (dynamic_internal_friction + eddy_visc)
        profile = jnp.cumsum(increment, axis=0)
        midpoint = profile - 0.5 * increment
        conduct = isobaric_caloric_constant * (dynamic_internal_friction / diffusivity_quotient + eddy_visc / prandtl_turb)
        conduction_impedance = lax.optimization_barrier(jnp.sum(spacing / conduct, axis=0))
        traction_power_addend = lax.optimization_barrier(jnp.sum(midpoint * spacing / conduct, axis=0))
        surface_enthalpy_rate = (fluid_kelvin - airfoil_surface_kelvin + tangential_traction * traction_power_addend) / conduction_impedance
        tangential_traction = tangential_traction * speed / profile[-1]
    return jnp.stack([100.0 * tangential_traction / (fluid_rho_value * speed * speed), 100.0 * surface_enthalpy_rate / (fluid_rho_value * isobaric_caloric_constant * speed)])

def reference(conserved_vector, occupied_patches, reading_volume, reading_surface, reading_elevation, airfoil_surface_kelvin):
    section_one = conserved_vector + time_step * full_tendency(conserved_vector)
    section_two = 0.75 * conserved_vector + 0.25 * (section_one + time_step * full_tendency(section_one))
    new_field = 1.0 / 3.0 * conserved_vector + 2.0 / 3.0 * (section_two + time_step * full_tendency(section_two))
    source = jnp.arange(DEVICES, dtype=jnp.int32)[:, None, None]
    span_cell = source // N_STREAM * CS + reading_volume // (CT * NP)
    column = source % N_STREAM * CT + reading_volume // NP % CT
    pitch_cell = reading_volume % NP
    picked = jnp.transpose(conserved_vector[:, span_cell, column, pitch_cell], (0, 2, 1, 3))
    owner_id = jnp.arange(DEVICES, dtype=jnp.int32)[:, None, None]
    target = jnp.where(reading_surface < 0, SURFACE_SLOTS, owner_id * FACES_DEV + reading_surface).astype(jnp.int32)
    surface_lookup = jnp.zeros((5, SURFACE_SLOTS), jnp.float32).at[:, target.reshape(-1)].set(picked.reshape(5, -1), mode='drop')
    face_ids = jnp.arange(SURFACE_SLOTS, dtype=jnp.int32)
    live_face = face_ids % FACES_DEV < TILE * occupied_patches[face_ids // FACES_DEV]
    filler = jnp.array([1.0, 0.4, 0.0, 0.0, 3.0], jnp.float32)[:, None]
    surface_lookup = jnp.where(live_face[None], surface_lookup, filler)
    arguments_given = jnp.concatenate([surface_lookup, reading_elevation[None], airfoil_surface_kelvin[None]], axis=0)
    blocks = jnp.transpose(arguments_given.reshape(7, DEVICES, FACES_DEV), (1, 0, 2))
    solved = lax.map(lambda block_data: surface_closure(block_data[:5], block_data[5], block_data[6]), blocks)
    face_flux = jnp.transpose(solved, (1, 0, 2)).reshape(2, SURFACE_SLOTS)
    return (new_field, jnp.where(live_face[None], face_flux, 0.0))
```

```python
import math

import jax
import jax.numpy as jnp
import numpy as np
from jax import lax
from jax.experimental import pallas as pl
from jax.experimental.pallas import tpu as pltpu
from jax.sharding import PartitionSpec as P

NPTS = 64
ITERS = 6
HALO = 3
LANES = 128
QUARTERS = 4
ROWS = 32

f32 = jnp.float32
bf16 = jnp.bfloat16


def split_bf16(x):
    hi = x.astype(bf16)
    rest = x - hi.astype(f32)
    mid = rest.astype(bf16)
    low = (rest - mid.astype(f32)).astype(bf16)
    return hi, mid, low


def gather_kernel(state, volume, out):
    cells = jnp.concatenate([volume[...], jnp.zeros((LANES, LANES - 8), jnp.int32)], axis=1)
    cells = jnp.transpose(cells.astype(f32))[:8].astype(jnp.int32)
    pitch = cells & 511
    row = cells >> 9
    lanes_iota = lax.broadcasted_iota(jnp.int32, (512, LANES), 0)
    hot = jnp.concatenate(
        [jnp.where(lanes_iota == pitch[k : k + 1], 1.0, 0.0).astype(bf16) for k in range(8)], axis=1
    )
    rows_iota = lax.broadcasted_iota(jnp.int32, (64, LANES), 0)
    masks = jnp.concatenate(
        [jnp.where(rows_iota == row[k : k + 1], 1.0, 0.0) for k in range(8)], axis=1
    )
    picked = []
    for c in range(5):
        hi, mid, low = split_bf16(state[c].reshape(64, 512))
        got = sum(
            lax.dot_general(part, hot, (((1,), (0,)), ((), ())), preferred_element_type=f32)
            for part in (low, mid, hi)
        )
        chosen = jnp.sum(got * masks, axis=0, keepdims=True)
        picked += [chosen[:, k * LANES : (k + 1) * LANES] for k in range(8)]
    table = jnp.concatenate(picked + [jnp.zeros((LANES - 40, LANES), f32)], axis=0)
    out[...] = jnp.transpose(table)


def gather_samples(state, volume):
    return pl.pallas_call(
        gather_kernel,
        out_shape=jax.ShapeDtypeStruct((LANES, LANES), f32),
        in_specs=[pl.BlockSpec(memory_space=pltpu.VMEM)] * 2,
        out_specs=pl.BlockSpec(memory_space=pltpu.VMEM),
        compiler_params=pltpu.CompilerParams(vmem_limit_bytes=40 * 2**20),
        cost_estimate=pl.CostEstimate(flops=10**9, bytes_accessed=10**6, transcendentals=0),
    )(state, volume)


_levels = np.exp(3.0 * np.arange(NPTS) / (NPTS - 1)) - 1.0
_levels = _levels / (math.exp(3.0) - 1.0)
_spacing = [float(v) for v in _levels[1:] - _levels[:-1]]
_middle = [float(v) for v in 0.5 * (_levels[1:] + _levels[:-1])]


def wall_kernel(tiles, received, surface, height, kelvin, out):
    table = jnp.transpose(received[...])
    target = surface[...]
    wide = jnp.concatenate([target, jnp.zeros((LANES, LANES - 8), jnp.int32)], axis=1)
    by_slot = jnp.transpose(wide.astype(f32))[:8].astype(jnp.int32)
    tile_of = by_slot >> 7
    tile_of = jnp.where(by_slot < 0, -1, tile_of)
    sub = lax.broadcasted_iota(jnp.int32, (8, LANES), 0)
    lane = lax.broadcasted_iota(jnp.int32, (LANES, LANES), 1)
    low_bits = target & 127
    hot = jnp.concatenate(
        [jnp.where(lane == low_bits[:, k : k + 1], 1.0, 0.0).astype(bf16) for k in range(8)], axis=0
    )
    rows = []
    for c in range(5):
        rows.append(
            jnp.concatenate(
                [
                    jnp.where(sub == tile_of[k : k + 1], table[c * 8 + k : c * 8 + k + 1], 0.0)
                    for k in range(8)
                ],
                axis=1,
            )
        )
    spread = jnp.concatenate(rows, axis=0)
    faces = sum(
        lax.dot_general(part, hot, (((1,), (0,)), ((), ())), preferred_element_type=f32)
        for part in reversed(split_bf16(spread))
    )
    live = sub < tiles[0]
    filler = (1.0, 0.4, 0.0, 0.0, 3.0)
    rho, mx, my, mz, energy = (
        jnp.where(live, faces[c * 8 : c * 8 + 8], filler[c]) for c in range(5)
    )
    h = height[...]
    wall = kelvin[...]
    power = mx * mx + my * my + mz * mz
    speed = jnp.sqrt(power) / rho
    temperature = 0.4 * (energy - 0.5 * power / rho) / rho
    tau = 0.002 * speed / h

    def viscosity(tau):
        friction = jnp.sqrt(tau / rho)
        a = rho * 0.41 * friction * h
        b = friction * rho * h * (-1.0 / (0.002 * 17.0))
        return a, b

    def eddy(a, b, j):
        damp = 1.0 - jnp.exp(b * _middle[j])
        return (a * _middle[j]) * (damp * damp)

    def step(_, tau):
        a, b = viscosity(tau)
        total = [jnp.zeros_like(tau) for _ in range(4)]
        for j in range(NPTS - 1):
            total[j % 4] = total[j % 4] + _spacing[j] / (0.002 + eddy(a, b, j))
        total = (total[0] + total[1]) + (total[2] + total[3])
        return tau * speed / (tau * h * total)

    tau = lax.fori_loop(0, ITERS - 1, step, tau)
    a, b = viscosity(tau)
    total = jnp.zeros_like(tau)
    impedance = jnp.zeros_like(tau)
    work = jnp.zeros_like(tau)
    for j in range(NPTS - 1):
        nu = eddy(a, b, j)
        increment = _spacing[j] / (0.002 + nu)
        total = total + increment
        part = _spacing[j] / (3.5 * (0.002 / 0.72) + (3.5 / 0.9) * nu)
        impedance = impedance + part
        work = work + (total - 0.5 * increment) * part
    scale = tau * h
    rate = (temperature - wall + tau * (scale * h * work)) / (h * impedance)
    tau = tau * speed / (scale * total)
    out[0] = jnp.where(live, 100.0 * tau / (rho * speed * speed), 0.0)
    out[1] = jnp.where(live, 100.0 * rate / (rho * 3.5 * speed), 0.0)


def wall_faces(tiles, received, surface, height, kelvin):
    return pl.pallas_call(
        wall_kernel,
        out_shape=jax.ShapeDtypeStruct((2, 8, LANES), f32),
        in_specs=[pl.BlockSpec(memory_space=pltpu.SMEM)]
        + [pl.BlockSpec(memory_space=pltpu.VMEM)] * 4,
        out_specs=pl.BlockSpec(memory_space=pltpu.VMEM),
        compiler_params=pltpu.CompilerParams(vmem_limit_bytes=40 * 2**20),
        cost_estimate=pl.CostEstimate(flops=10**8, bytes_accessed=10**6, transcendentals=10**6),
    )(tiles, received, surface, height, kelvin)


def pack_kernel(place, state, first, second, out_first, out_second):
    span_odd = place[0] % 2
    stream_odd = place[1] % 2

    def rows(src, plane, ext, c, low_out, high_out):
        for q in range(QUARTERS):
            at = ((c * 10 + ext) * QUARTERS + q) * HALO
            lanes = slice(q * LANES, (q + 1) * LANES)
            low_out[pl.ds(at, HALO), :] = src[c, plane, 0:HALO, lanes]
            high_out[pl.ds(at, HALO), :] = src[c, plane, 16 - HALO : 16, lanes]

    def fill(before, after, low_out, high_out):
        def body(c, _):
            for p in range(HALO):
                rows(before, p, p, c, low_out, high_out)
                rows(after, p, 7 + p, c, low_out, high_out)
            for p in range(4):
                rows(state, p, HALO + p, c, low_out, high_out)
            return 0

        lax.fori_loop(0, 5, body, 0)

    for so in range(2):
        for to in range(2):

            @pl.when((span_odd == so) & (stream_odd == to))
            def _():
                before, after = (first, second) if so else (second, first)
                low_out, high_out = (out_first, out_second) if to else (out_second, out_first)
                fill(before, after, low_out, high_out)


def pack_rows(place, state, first, second):
    shape = jax.ShapeDtypeStruct((5 * 10 * QUARTERS * HALO, LANES), f32)
    return pl.pallas_call(
        pack_kernel,
        out_shape=(shape, shape),
        in_specs=[pl.BlockSpec(memory_space=pltpu.SMEM)]
        + [pl.BlockSpec(memory_space=pltpu.VMEM)] * 3,
        out_specs=(pl.BlockSpec(memory_space=pltpu.VMEM),) * 2,
        compiler_params=pltpu.CompilerParams(vmem_limit_bytes=40 * 2**20),
        cost_estimate=pl.CostEstimate(flops=10**6, bytes_accessed=2 * 10**6, transcendentals=0),
    )(place, state, first, second)


def swap(x, axis, parity):
    size = lax.axis_size(axis)
    pairs = []
    for i in range(parity, size - 1, 2):
        pairs += [(i, i + 1), (i + 1, i)]
    return lax.ppermute(x, axis, pairs)


def field_kernel(place, state, span_a, span_b, stream_a, stream_b, out, e0, e1, e2, der, gspan, gstream):
    span_at, stream_at = place[0], place[1]
    span_odd, stream_odd = span_at % 2, stream_at % 2
    lane_id = lax.broadcasted_iota(jnp.int32, (QUARTERS, 8, LANES), 2)
    is_last, is_first = lane_id == LANES - 1, lane_id == 0

    def put(src, plane, ext, c):
        for q in range(QUARTERS):
            for i in range(2):
                e0[c, ext, q, pl.ds(HALO + 8 * i, 8), :] = src[
                    c, plane, 8 * i : 8 * i + 8, q * LANES : (q + 1) * LANES
                ]

    def own(c, _):
        for p in range(4):
            put(state, p, HALO + p, c)
        return 0

    lax.fori_loop(0, 5, own, 0)

    def halo_planes(before, after):
        def body(c, _):
            for p in range(HALO):
                put(before, p, p, c)
                put(after, p, 7 + p, c)
            return 0

        lax.fori_loop(0, 5, body, 0)

    def halo_rows(before, after):
        def body(i, _):
            c, ext = i // 10, i % 10
            for q in range(QUARTERS):
                at = (i * QUARTERS + q) * HALO
                e0[c, ext, q, pl.ds(0, HALO), :] = before[pl.ds(at, HALO), :]
                e0[c, ext, q, pl.ds(HALO + 16, HALO), :] = after[pl.ds(at, HALO), :]
            return 0

        lax.fori_loop(0, 50, body, 0)

    @pl.when(span_odd == 0)
    def _():
        halo_planes(span_b, span_a)

    @pl.when(span_odd == 1)
    def _():
        halo_planes(span_a, span_b)

    @pl.when(stream_odd == 0)
    def _():
        halo_rows(stream_b, stream_a)

    @pl.when(stream_odd == 1)
    def _():
        halo_rows(stream_a, stream_b)

    def clamp(e):
        def plane(dst, src):
            for c in range(5):
                for i in range(3):
                    e[c, dst, :, pl.ds(8 * i, 8), :] = e[c, src, :, pl.ds(8 * i, 8), :]

        def row(dst, src):
            def body(p, _):
                for c in range(5):
                    for q in range(QUARTERS):
                        e[c, p, q, pl.ds(dst, 1), :] = e[c, p, q, pl.ds(src, 1), :]
                return 0

            lax.fori_loop(0, 10, body, 0)

        @pl.when(span_at == 0)
        def _():
            plane(2, 3)

        @pl.when(span_at == place[2] - 1)
        def _():
            plane(7, 6)

        @pl.when(stream_at == 0)
        def _():
            row(2, 3)

        @pl.when(stream_at == place[3] - 1)
        def _():
            row(19, 18)

    normal = ((0, 1, 2, 6, 9), (1, 3, 4, 7, 10), (2, 4, 5, 8, 11))

    def stage(src, lo, hi, r0, chunks, finish):
        starts = [r0 - 1 + 8 * i for i in range(3)]

        def primitive(p):
            for r in starts:
                at = pl.ds(r, 8)
                rho, m1, m2, m3, energy = (src[c, p, :, at, :] for c in range(5))
                inv = pl.reciprocal(rho, approx=True)
                inv = inv * (2.0 - rho * inv)
                v1, v2, v3 = m1 * inv, m2 * inv, m3 * inv
                t11, t22, t33 = m1 * v1, m2 * v2, m3 * v3
                pressure = 0.4 * energy - 0.2 * (t11 + t22 + t33)
                der[0, p, :, at, :] = t11 + pressure
                der[3, p, :, at, :] = t22 + pressure
                der[5, p, :, at, :] = t33 + pressure
                der[1, p, :, at, :] = m1 * v2
                der[2, p, :, at, :] = m1 * v3
                der[4, p, :, at, :] = m2 * v3
                total = energy + pressure
                der[6, p, :, at, :] = total * v1
                der[7, p, :, at, :] = total * v2
                der[8, p, :, at, :] = total * v3
                square = 1.4 * pressure * inv
                sound = square * lax.rsqrt(square) + 0.04
                der[9, p, :, at, :] = jnp.abs(v1) + sound
                der[10, p, :, at, :] = jnp.abs(v2) + sound
                der[11, p, :, at, :] = jnp.abs(v3) + sound

        def flux(c, k, p, at):
            if c == 0:
                return src[1 + k, p, :, at, :]
            return der[normal[k][c - 1], p, :, at, :]

        def span_faces(p, at, c, coef):
            g = coef * (src[c, p + 1, :, at, :] - src[c, p, :, at, :])
            return g - (flux(c, 0, p, at) + flux(c, 0, p + 1, at))

        def after(x):
            r = pltpu.roll(x, LANES - 1, 2)
            return jnp.where(is_last, jnp.concatenate([r[1:], r[:1]], axis=0), r)

        def before(x):
            r = pltpu.roll(x, 1, 2)
            return jnp.where(is_first, jnp.concatenate([r[-1:], r[:-1]], axis=0), r)

        primitive(lo - 1)
        primitive(lo)
        for i in range(chunks):
            at = pl.ds(r0 + 8 * i, 8)
            coef = jnp.maximum(der[9, lo - 1, :, at, :], der[9, lo, :, at, :])
            for c in range(5):
                gspan[c, i] = span_faces(lo - 1, at, c, coef - 0.04 if c == 0 else coef)

        def plane(p, _):
            primitive(p + 1)
            for r in starts:
                at, up = pl.ds(r, 8), pl.ds(r + 1, 8)
                coef = jnp.maximum(der[10, p, :, at, :], der[10, p, :, up, :])
                for c in range(5):
                    g = (coef - 0.04 if c == 0 else coef) * (src[c, p, :, up, :] - src[c, p, :, at, :])
                    gstream[c, :, at, :] = g - (flux(c, 1, p, at) + flux(c, 1, p, up))
            for i in range(chunks):
                r = r0 + 8 * i
                at, down = pl.ds(r, 8), pl.ds(r - 1, 8)
                coef_span = jnp.maximum(der[9, p, :, at, :], der[9, p + 1, :, at, :])
                wave = der[11, p, :, at, :]
                coef_pitch = jnp.maximum(wave, after(wave))
                for c in range(5):
                    u = src[c, p, :, at, :]
                    g_up = span_faces(p, at, c, coef_span - 0.04 if c == 0 else coef_span)
                    acc = g_up - gspan[c, i]
                    gspan[c, i] = g_up
                    acc = acc + (gstream[c, :, at, :] - gstream[c, :, down, :])
                    f = flux(c, 2, p, at)
                    g = (coef_pitch - 0.04 if c == 0 else coef_pitch) * (after(u) - u)
                    g = g - (f + after(f))
                    acc = acc + (g - before(g))
                    finish(c, p, r, i, u, acc)
            return 0

        lax.fori_loop(lo, hi + 1, plane, 0)

    def finish_one(c, p, r, i, u, acc):
        e1[c, p, :, pl.ds(r, 8), :] = u + 0.05 * acc

    def finish_two(c, p, r, i, u, acc):
        e2[c, p, :, pl.ds(r, 8), :] = 0.75 * e0[c, p, :, pl.ds(r, 8), :] + (0.25 * u + 0.0125 * acc)

    def finish_three(c, p, r, i, u, acc):
        new = (1.0 / 3.0) * e0[c, p, :, pl.ds(r, 8), :] + ((2.0 / 3.0) * u + (0.1 / 3.0) * acc)
        for q in range(QUARTERS):
            out[c, p - HALO, 8 * i : 8 * i + 8, q * LANES : (q + 1) * LANES] = new[q]

    clamp(e0)
    stage(e0, 1, 8, 1, 3, finish_one)
    clamp(e1)
    stage(e1, 2, 7, 2, 3, finish_two)
    clamp(e2)
    stage(e2, 3, 6, 3, 2, finish_three)


def advance_field(place, state, span_a, span_b, stream_a, stream_b):
    block = pltpu.VMEM((5, 10, QUARTERS, ROWS, LANES), f32)
    return pl.pallas_call(
        field_kernel,
        out_shape=jax.ShapeDtypeStruct(state.shape, f32),
        in_specs=[pl.BlockSpec(memory_space=pltpu.SMEM)]
        + [pl.BlockSpec(memory_space=pltpu.VMEM)] * 5,
        out_specs=pl.BlockSpec(memory_space=pltpu.VMEM),
        scratch_shapes=[
            block,
            block,
            block,
            pltpu.VMEM((12, 10, QUARTERS, ROWS, LANES), f32),
            pltpu.VMEM((5, 3, QUARTERS, 8, LANES), f32),
            pltpu.VMEM((5, QUARTERS, ROWS, LANES), f32),
        ],
        compiler_params=pltpu.CompilerParams(vmem_limit_bytes=48 * 2**20),
        cost_estimate=pl.CostEstimate(flops=3 * 10**7, bytes_accessed=4 * 10**6, transcendentals=10**5),
    )(place, state, span_a, span_b, stream_a, stream_b)


def per_device(state, tiles, volume, surface, height, kelvin):
    span_at, stream_at = lax.axis_index("span"), lax.axis_index("stream")
    place = jnp.stack(
        [span_at, stream_at, lax.axis_size("span"), lax.axis_size("stream")]
    ).astype(jnp.int32)
    span_odd = span_at % 2
    planes = state.shape[1]
    top = planes - HALO
    first = lax.dynamic_slice_in_dim(state, (1 - span_odd) * top, HALO, 1)
    second = lax.dynamic_slice_in_dim(state, span_odd * top, HALO, 1)
    span_a, span_b = swap(first, "span", 0), swap(second, "span", 1)

    outgoing = gather_samples(state, volume[0])
    received = lax.all_to_all(outgoing, ("span", "stream"), 0, 0, tiled=True)

    pack_a, pack_b = pack_rows(place, state, span_a, span_b)
    stream_a, stream_b = swap(pack_a, "stream", 0), swap(pack_b, "stream", 1)

    flux = wall_faces(tiles, received, surface[0], height.reshape(8, LANES), kelvin.reshape(8, LANES))
    field = advance_field(place, state, span_a, span_b, stream_a, stream_b)
    return field, flux.reshape(2, -1)


def solution(mesh):
    in_specs = (
        P(None, "span", "stream", None),
        P(("span", "stream")),
        P(("span", "stream"), None, None),
        P(("span", "stream"), None, None),
        P(("span", "stream")),
        P(("span", "stream")),
    )
    out_specs = (P(None, "span", "stream", None), P(None, ("span", "stream")))
    return jax.shard_map(per_device, mesh=mesh, in_specs=in_specs, out_specs=out_specs, check_vma=False)
```

```python
import math

import jax
import jax.numpy as jnp
import numpy as np
from jax import lax
from jax.experimental import pallas as pl
from jax.experimental.pallas import tpu as pltpu
from jax.sharding import PartitionSpec as P

NPTS = 64
ITERS = 6
HALO = 3
LANES = 128
QUARTERS = 4
ROWS = 32

f32 = jnp.float32
bf16 = jnp.bfloat16


def split_bf16(x, parts):
    out = []
    for _ in range(parts):
        out.append(x.astype(bf16))
        x = x - out[-1].astype(f32)
    return out


def gather_kernel(view, volume, out, cells, table, halves):
    wide = jnp.concatenate([volume[...], jnp.zeros((LANES, LANES - 8), jnp.int32)], axis=1)
    cells[...] = jnp.transpose(wide.astype(f32))[:8].astype(jnp.int32)
    for c in range(5):
        rows = [jnp.concatenate([view[c, a, j] for j in range(QUARTERS)], axis=1) for a in range(4)]
        put_halves(halves, c, jnp.concatenate(rows, axis=0))
    table[...] = jnp.zeros((LANES, LANES), f32)
    pitch_of = lax.broadcasted_iota(jnp.int32, (512, LANES), 0)
    row_of = lax.broadcasted_iota(jnp.int32, (64, LANES), 0)

    def pair(n, _):
        slots = [cells[pl.ds(2 * n + k, 1), :] for k in range(2)]
        hot = jnp.concatenate(
            [
                jnp.where(pitch_of == ((cell & 3) << 7) + ((cell & 511) >> 2), 1.0, 0.0).astype(bf16)
                for cell in slots
            ],
            axis=1,
        )
        got = lax.dot_general(
            halves[...], hot, (((1,), (0,)), ((), ())), preferred_element_type=f32
        )
        for k, cell in enumerate(slots):
            here = row_of == (cell >> 9)
            for c in range(5):
                lanes = slice(k * LANES, (k + 1) * LANES)
                both = got[c * 64 : c * 64 + 64, lanes] + got[320 + c * 64 : 384 + c * 64, lanes]
                table[pl.ds(c * 8 + 2 * n + k, 1), :] = jnp.sum(
                    jnp.where(here, both, 0.0), axis=0, keepdims=True
                )
        return 0

    lax.fori_loop(0, 4, pair, 0)
    out[...] = jnp.transpose(table[...])


def gather_samples(view, volume):
    return pl.pallas_call(
        gather_kernel,
        out_shape=jax.ShapeDtypeStruct((LANES, LANES), f32),
        in_specs=[pl.BlockSpec(memory_space=pltpu.VMEM)] * 2,
        out_specs=pl.BlockSpec(memory_space=pltpu.VMEM),
        scratch_shapes=[
            pltpu.VMEM((8, LANES), jnp.int32),
            pltpu.VMEM((LANES, LANES), f32),
            pltpu.VMEM((640, 512), bf16),
        ],
        compiler_params=pltpu.CompilerParams(vmem_limit_bytes=40 * 2**20),
        cost_estimate=pl.CostEstimate(flops=10**9, bytes_accessed=10**6, transcendentals=0),
    )(view, volume)


_levels = np.exp(3.0 * np.arange(NPTS) / (NPTS - 1)) - 1.0
_levels = _levels / (math.exp(3.0) - 1.0)
_spacing = [float(v) for v in _levels[1:] - _levels[:-1]]
_middle = [float(v) for v in 0.5 * (_levels[1:] + _levels[:-1])]


def face_kernel(tiles, surface, height, kelvin, hot, tile_of, live, h, wall):
    target = surface[...]
    lane = lax.broadcasted_iota(jnp.int32, (LANES, LANES), 1)
    low_bits = target & 127
    for k in range(8):
        hot[pl.ds(k * LANES, LANES), :] = jnp.where(lane == low_bits[:, k : k + 1], 1.0, 0.0).astype(bf16)
    wide = jnp.concatenate([target, jnp.zeros((LANES, LANES - 8), jnp.int32)], axis=1)
    by_slot = jnp.transpose(wide.astype(f32))[:8].astype(jnp.int32)
    tile_of[...] = jnp.where(by_slot < 0, -1, by_slot >> 7)
    live[...] = jnp.where(lax.broadcasted_iota(jnp.int32, (8, LANES), 0) < tiles[0], 1.0, 0.0)
    h[...] = height[...]
    wall[...] = kelvin[...]


def face_tables(tiles, surface, height, kelvin):
    tile = jax.ShapeDtypeStruct((8, LANES), f32)
    return pl.pallas_call(
        face_kernel,
        out_shape=(
            jax.ShapeDtypeStruct((8 * LANES, LANES), bf16),
            jax.ShapeDtypeStruct((8, LANES), jnp.int32),
            tile,
            tile,
            tile,
        ),
        in_specs=[pl.BlockSpec(memory_space=pltpu.SMEM)]
        + [pl.BlockSpec(memory_space=pltpu.VMEM)] * 3,
        out_specs=(pl.BlockSpec(memory_space=pltpu.VMEM),) * 5,
        compiler_params=pltpu.CompilerParams(vmem_limit_bytes=40 * 2**20),
        cost_estimate=pl.CostEstimate(flops=10**6, bytes_accessed=10**6, transcendentals=0),
    )(tiles, surface, height, kelvin)


def wall_kernel(received, hot, tile_of, alive, height, kelvin, _mark, out):
    table = jnp.transpose(received[...])
    sub = lax.broadcasted_iota(jnp.int32, (8, LANES), 0)
    here = [sub == tile_of[k : k + 1] for k in range(8)]
    spread = jnp.concatenate(
        [
            jnp.concatenate(
                [jnp.where(here[k], table[c * 8 + k : c * 8 + k + 1], 0.0) for k in range(8)], axis=1
            )
            for c in range(5)
        ],
        axis=0,
    )
    parts = jnp.concatenate(split_bf16(spread, 2), axis=0)
    faces = lax.dot_general(parts, hot[...], (((1,), (0,)), ((), ())), preferred_element_type=f32)
    faces = faces[40:] + faces[:40]
    live = alive[...] > 0.5
    filler = (1.0, 0.4, 0.0, 0.0, 3.0)
    rho, mx, my, mz, energy = (
        jnp.where(live, faces[c * 8 : c * 8 + 8], filler[c]) for c in range(5)
    )
    h = height[...]
    wall = kelvin[...]
    power = mx * mx + my * my + mz * mz
    speed = jnp.sqrt(power) / rho
    temperature = 0.4 * (energy - 0.5 * power / rho) / rho
    tau = 0.002 * speed / h

    def viscosity(tau):
        friction = jnp.sqrt(tau / rho)
        a = rho * 0.41 * friction * h
        b = friction * rho * h * (-1.0 / (0.002 * 17.0))
        return a, b

    def eddy(a, b, j):
        damp = 1.0 - jnp.exp(b * _middle[j])
        return (a * _middle[j]) * (damp * damp)

    def step(_, tau):
        a, b = viscosity(tau)
        total = [jnp.zeros_like(tau) for _ in range(4)]
        for j in range(NPTS - 1):
            total[j % 4] = total[j % 4] + _spacing[j] / (0.002 + eddy(a, b, j))
        total = (total[0] + total[1]) + (total[2] + total[3])
        return tau * speed / (tau * h * total)

    tau = lax.fori_loop(0, ITERS - 1, step, tau)
    a, b = viscosity(tau)
    total = jnp.zeros_like(tau)
    impedance = jnp.zeros_like(tau)
    work = jnp.zeros_like(tau)
    for j in range(NPTS - 1):
        nu = eddy(a, b, j)
        increment = _spacing[j] / (0.002 + nu)
        total = total + increment
        part = _spacing[j] / (3.5 * (0.002 / 0.72) + (3.5 / 0.9) * nu)
        impedance = impedance + part
        work = work + (total - 0.5 * increment) * part
    scale = tau * h
    rate = (temperature - wall + tau * (scale * h * work)) / (h * impedance)
    tau = tau * speed / (scale * total)
    friction = jnp.where(live, 100.0 * tau / (rho * speed * speed), 0.0)
    heat = jnp.where(live, 100.0 * rate / (rho * 3.5 * speed), 0.0)
    for i in range(8):
        out[0:1, i * LANES : (i + 1) * LANES] = friction[i : i + 1]
        out[1:2, i * LANES : (i + 1) * LANES] = heat[i : i + 1]


def wall_faces(received, tables, mark):
    return pl.pallas_call(
        wall_kernel,
        out_shape=jax.ShapeDtypeStruct((2, 8 * LANES), f32),
        in_specs=[pl.BlockSpec(memory_space=pltpu.VMEM)] * 6 + [pl.BlockSpec(memory_space=pl.ANY)],
        out_specs=pl.BlockSpec(memory_space=pltpu.VMEM),
        compiler_params=pltpu.CompilerParams(vmem_limit_bytes=40 * 2**20),
        cost_estimate=pl.CostEstimate(flops=10**8, bytes_accessed=10**6, transcendentals=10**6),
    )(received, *tables, mark)


def pitch_map(across):
    p = lax.broadcasted_iota(jnp.int32, (512, 512), 1 if across else 0)
    n = lax.broadcasted_iota(jnp.int32, (512, 512), 0 if across else 1)
    return jnp.where(p == 4 * (n & 127) + (n >> 7), 1.0, 0.0).astype(bf16)


def put_halves(halves, c, rows):
    hi, low = split_bf16(rows, 2)
    halves[pl.ds(c * 64, 64), :] = hi
    halves[pl.ds(320 + c * 64, 64), :] = low


def remap(halves, table):
    got = lax.dot_general(halves[...], table, (((1,), (0,)), ((), ())), preferred_element_type=f32)
    return got[:320] + got[320:]


def view_kernel(state, view, first, second, halves):
    table = pitch_map(False)
    odd = lax.axis_index("stream") % 2
    row_first = (1 - odd) * (16 - HALO)
    row_second = odd * (16 - HALO)
    for c in range(5):
        put_halves(halves, c, state[c].reshape(64, 512))
    x = remap(halves, table)
    for c in range(5):
        for a in range(4):
            for j in range(QUARTERS):
                at = 64 * c + 16 * a
                view[c, a, j] = x[at : at + 16, j * LANES : (j + 1) * LANES]
    for c in range(5):
        for a in range(4):
            for j in range(QUARTERS):
                at = ((c * 4 + a) * QUARTERS + j) * HALO
                first[pl.ds(at, HALO), :] = view[c, a, j, pl.ds(row_first, HALO), :]
                second[pl.ds(at, HALO), :] = view[c, a, j, pl.ds(row_second, HALO), :]


def view_field(state):
    side = jax.ShapeDtypeStruct((5 * 4 * QUARTERS * HALO, LANES), f32)
    return pl.pallas_call(
        view_kernel,
        out_shape=(jax.ShapeDtypeStruct((5, 4, QUARTERS, 16, LANES), f32), side, side),
        in_specs=[pl.BlockSpec(memory_space=pltpu.VMEM)],
        out_specs=(pl.BlockSpec(memory_space=pltpu.VMEM),) * 3,
        scratch_shapes=[pltpu.VMEM((640, 512), bf16)],
        compiler_params=pltpu.CompilerParams(vmem_limit_bytes=40 * 2**20),
        cost_estimate=pl.CostEstimate(flops=10**9, bytes_accessed=3 * 10**6, transcendentals=0),
    )(state)


REACH = ((1, -2, 20, 0), (2, -1, 18, 20), (3, 0, 16, 38))
SIDE = 54


def pack_kernel(view, stream_a, stream_b, _samples, first, second):
    span_odd = lax.axis_index("span") % 2
    stream_odd = lax.axis_index("stream") % 2

    def fill(before, after):
        def body(c, _):
            for out, high in ((first, span_odd == 0), (second, span_odd == 1)):
                for distance, _, count, base in REACH:
                    plane = jnp.where(high, 4 - distance, distance - 1)
                    extra = HALO - distance
                    for j in range(QUARTERS):
                        at = (c * QUARTERS + j) * SIDE + base
                        side = ((c * 4 + plane) * QUARTERS + j) * HALO
                        for i in range(2):
                            out[pl.ds(at + extra + 8 * i, 8), :] = view[c, plane, j, pl.ds(8 * i, 8), :]
                        if extra:
                            out[pl.ds(at, extra), :] = before[pl.ds(side + distance, extra), :]
                            out[pl.ds(at + extra + 16, extra), :] = after[pl.ds(side, extra), :]
            return 0

        lax.fori_loop(0, 5, body, 0)

    @pl.when(stream_odd == 0)
    def _():
        fill(stream_b, stream_a)

    @pl.when(stream_odd == 1)
    def _():
        fill(stream_a, stream_b)


def pack_planes(view, stream_a, stream_b, samples):
    shape = jax.ShapeDtypeStruct((5 * QUARTERS * SIDE, LANES), f32)
    return pl.pallas_call(
        pack_kernel,
        out_shape=(shape, shape),
        in_specs=[pl.BlockSpec(memory_space=pltpu.VMEM)] * 3 + [pl.BlockSpec(memory_space=pl.ANY)],
        out_specs=(pl.BlockSpec(memory_space=pltpu.VMEM),) * 2,
        compiler_params=pltpu.CompilerParams(vmem_limit_bytes=40 * 2**20),
        cost_estimate=pl.CostEstimate(flops=10**6, bytes_accessed=2 * 10**6, transcendentals=0),
    )(view, stream_a, stream_b, samples)


def swap(x, axis, parity):
    spans, streams = lax.axis_size("span"), lax.axis_size("stream")

    def partner(i, n):
        other = i + 1 if i % 2 == parity else i - 1
        return other if 0 <= other < n else None

    pairs = []
    for a in range(spans):
        for b in range(streams):
            if axis == "span":
                other = partner(a, spans)
                there = (a, b ^ 1) if other is None else (other, b)
            else:
                other = partner(b, streams)
                there = (a ^ 1, b) if other is None else (a, other)
            pairs.append((a * streams + b, there[0] * streams + there[1]))
    return lax.ppermute(x, ("span", "stream"), pairs)


def field_kernel(
    state, span_a, span_b, stream_a, stream_b, _tile_of, out, mark, e0, e1, e2, der, gspan, gstream, halves
):
    span_at, stream_at = lax.axis_index("span"), lax.axis_index("stream")
    span_odd, stream_odd = span_at % 2, stream_at % 2

    def own(c, _):
        for p in range(4):
            for i in range(2):
                e0[c, HALO + p, :, pl.ds(HALO + 8 * i, 8), :] = state[c, p, :, pl.ds(8 * i, 8), :]
        return 0

    lax.fori_loop(0, 5, own, 0)

    def halo_rows(before, after):
        def body(c, _):
            for p in range(4):
                for j in range(QUARTERS):
                    at = ((c * 4 + p) * QUARTERS + j) * HALO
                    e0[c, HALO + p, j, pl.ds(0, HALO), :] = before[pl.ds(at, HALO), :]
                    e0[c, HALO + p, j, pl.ds(HALO + 16, HALO), :] = after[pl.ds(at, HALO), :]
            return 0

        lax.fori_loop(0, 5, body, 0)

    def halo_planes(before, after):
        def body(c, _):
            for src, high in ((before, False), (after, True)):
                for distance, row, count, base in REACH:
                    plane = 6 + distance if high else HALO - distance
                    for j in range(QUARTERS):
                        at = (c * QUARTERS + j) * SIDE + base
                        for i in range(0, count, 8):
                            n = min(8, count - i)
                            e0[c, plane, j, pl.ds(HALO + row + i, n), :] = src[pl.ds(at + i, n), :]
            return 0

        lax.fori_loop(0, 5, body, 0)

    @pl.when(stream_odd == 0)
    def _():
        halo_rows(stream_b, stream_a)

    @pl.when(stream_odd == 1)
    def _():
        halo_rows(stream_a, stream_b)

    @pl.when(span_odd == 0)
    def _():
        halo_planes(span_b, span_a)

    @pl.when(span_odd == 1)
    def _():
        halo_planes(span_a, span_b)

    def clamp(e):
        def plane(dst, src):
            for c in range(5):
                for i in range(3):
                    e[c, dst, :, pl.ds(8 * i, 8), :] = e[c, src, :, pl.ds(8 * i, 8), :]

        def row(dst, src):
            def body(p, _):
                for c in range(5):
                    for q in range(QUARTERS):
                        e[c, p, q, pl.ds(dst, 1), :] = e[c, p, q, pl.ds(src, 1), :]
                return 0

            lax.fori_loop(0, 10, body, 0)

        @pl.when(span_at == 0)
        def _():
            plane(2, 3)

        @pl.when(span_at == lax.axis_size("span") - 1)
        def _():
            plane(7, 6)

        @pl.when(stream_at == 0)
        def _():
            row(2, 3)

        @pl.when(stream_at == lax.axis_size("stream") - 1)
        def _():
            row(19, 18)

    normal = ((0, 1, 2, 6), (1, 3, 4, 7), (2, 4, 5, 8))

    def primitive(u):
        rho, m1, m2, m3, energy = u
        inv = pl.reciprocal(rho, approx=True)
        inv = inv * (2.0 - rho * inv)
        v1, v2, v3 = m1 * inv, m2 * inv, m3 * inv
        t11, t22, t33 = m1 * v1, m2 * v2, m3 * v3
        pressure = 0.4 * energy - 0.2 * (t11 + t22 + t33)
        total = energy + pressure
        square = 1.4 * pressure * inv
        sound = square * lax.rsqrt(square) + 0.04
        return [
            t11 + pressure,
            m1 * v2,
            m1 * v3,
            t22 + pressure,
            m2 * v3,
            t33 + pressure,
            total * v1,
            total * v2,
            total * v3,
            jnp.abs(v1) + sound,
            jnp.abs(v2) + sound,
            jnp.abs(v3) + sound,
        ]

    def fluxes(u, d, k):
        return [u[1 + k]] + [d[i] for i in normal[k]]

    def faces(low, high, low_flux, high_flux, coef):
        return [
            (coef - 0.04 if c == 0 else coef) * (high[c] - low[c]) - (low_flux[c] + high_flux[c])
            for c in range(5)
        ]

    def after(x):
        return jnp.concatenate([x[1:], pltpu.roll(x[:1], LANES - 1, 2)], axis=0)

    def before(x):
        return jnp.concatenate([pltpu.roll(x[-1:], 1, 2), x[:-1]], axis=0)

    def stage(src, lo, hi, r0, finish):
        starts = [r0 - 1 + 8 * i for i in range(3)]

        def cells(p, at):
            return [src[c, p, :, at, :] for c in range(5)]

        def load_der(p, at, which):
            return {n: der[n, p, :, at, :] for n in which}

        def fill(p, at):
            u = cells(p, at)
            d = primitive(u)
            for n in range(12):
                der[n, p, :, at, :] = d[n]
            return u, d

        for i, r in enumerate(starts):
            at = pl.ds(r, 8)
            u0, d0 = fill(lo - 1, at)
            u1, d1 = fill(lo, at)
            g = faces(u0, u1, fluxes(u0, d0, 0), fluxes(u1, d1, 0), jnp.maximum(d0[9], d1[9]))
            for c in range(5):
                gspan[c, i] = g[c]

        def plane(p, _):
            for r in starts:
                fill(p + 1, pl.ds(r, 8))
            for i, r in enumerate(starts):
                at, up, down = pl.ds(r, 8), pl.ds(r + 1, 8), pl.ds(r - 1 + 8, 8)

                def wave(n, q, rows):
                    return der[n, q, :, rows, :]

                here = wave(11, p, at)
                coefs = [
                    jnp.maximum(wave(9, p, at), wave(9, p + 1, at)),
                    jnp.maximum(wave(10, p, at), wave(10, p, up)),
                    jnp.maximum(here, after(here)),
                ]

                def flux(c, k, q, rows):
                    return src[1 + k, q, :, rows, :] if c == 0 else der[normal[k][c - 1], q, :, rows, :]

                for c in range(5):
                    use = [v - 0.04 for v in coefs] if c == 0 else coefs
                    u = src[c, p, :, at, :]
                    g = use[0] * (src[c, p + 1, :, at, :] - u) - (flux(c, 0, p, at) + flux(c, 0, p + 1, at))
                    acc = g - gspan[c, i]
                    gspan[c, i] = g
                    g = use[1] * (src[c, p, :, up, :] - u) - (flux(c, 1, p, at) + flux(c, 1, p, up))
                    gstream[c, :, pl.ds(r + 8, 8), :] = g
                    acc = acc + (g - gstream[c, :, down, :])
                    f = flux(c, 2, p, at)
                    g = use[2] * (after(u) - u) - (f + after(f))
                    finish(c, p, r, i, u, acc + (g - before(g)))
            return 0

        lax.fori_loop(lo, hi + 1, plane, 0)

    def finish_one(c, p, r, i, u, acc):
        e1[c, p, :, pl.ds(r, 8), :] = u + 0.05 * acc

    def finish_two(c, p, r, i, u, acc):
        e2[c, p, :, pl.ds(r, 8), :] = 0.75 * e0[c, p, :, pl.ds(r, 8), :] + (0.25 * u + 0.0125 * acc)

    def finish_three(c, p, r, i, u, acc):
        new = (1.0 / 3.0) * e0[c, p, :, pl.ds(r, 8), :] + ((2.0 / 3.0) * u + (0.1 / 3.0) * acc)
        e1[c, p, :, pl.ds(r, 8), :] = new

    clamp(e0)
    stage(e0, 1, 8, 1, finish_one)
    clamp(e1)
    stage(e1, 2, 7, 2, finish_two)
    clamp(e2)
    stage(e2, 3, 6, 3, finish_three)

    mark[...] = jnp.zeros((8, LANES), f32)
    for c in range(5):
        rows = [
            jnp.concatenate([e1[c, HALO + p, j, pl.ds(HALO, 16), :] for j in range(QUARTERS)], axis=1)
            for p in range(4)
        ]
        put_halves(halves, c, jnp.concatenate(rows, axis=0))
    new = remap(halves, pitch_map(True))
    for c in range(5):
        for p in range(4):
            out[c, p] = new[64 * c + 16 * p : 64 * c + 16 * p + 16]


def advance_field(view, span_a, span_b, stream_a, stream_b, tile_of):
    block = pltpu.VMEM((5, 10, QUARTERS, ROWS, LANES), f32)
    return pl.pallas_call(
        field_kernel,
        out_shape=(
            jax.ShapeDtypeStruct((5, 4, 16, 512), f32),
            jax.ShapeDtypeStruct((8, LANES), f32),
        ),
        in_specs=[pl.BlockSpec(memory_space=pltpu.VMEM)] * 5 + [pl.BlockSpec(memory_space=pl.ANY)],
        out_specs=(pl.BlockSpec(memory_space=pltpu.VMEM),) * 2,
        scratch_shapes=[
            block,
            block,
            block,
            pltpu.VMEM((12, 10, QUARTERS, ROWS, LANES), f32),
            pltpu.VMEM((5, 3, QUARTERS, 8, LANES), f32),
            pltpu.VMEM((5, QUARTERS, ROWS + 8, LANES), f32),
            pltpu.VMEM((640, 512), bf16),
        ],
        compiler_params=pltpu.CompilerParams(vmem_limit_bytes=48 * 2**20),
        cost_estimate=pl.CostEstimate(flops=3 * 10**7, bytes_accessed=4 * 10**6, transcendentals=10**5),
    )(view, span_a, span_b, stream_a, stream_b, tile_of)


def per_device(state, tiles, volume, surface, height, kelvin):
    view, first, second = view_field(state)
    stream_a, stream_b = swap(first, "stream", 0), swap(second, "stream", 1)

    outgoing = gather_samples(view, volume[0])
    received = lax.all_to_all(outgoing, ("span", "stream"), 0, 0, tiled=True)

    first, second = pack_planes(view, stream_a, stream_b, outgoing)
    span_a, span_b = swap(first, "span", 0), swap(second, "span", 1)
    tables = face_tables(tiles, surface[0], height.reshape(8, LANES), kelvin.reshape(8, LANES))
    field, mark = advance_field(view, span_a, span_b, stream_a, stream_b, tables[1])
    return field, wall_faces(received, tables, mark)


def solution(mesh):
    in_specs = (
        P(None, "span", "stream", None),
        P(("span", "stream")),
        P(("span", "stream"), None, None),
        P(("span", "stream"), None, None),
        P(("span", "stream")),
        P(("span", "stream")),
    )
    out_specs = (P(None, "span", "stream", None), P(None, ("span", "stream")))
    return jax.shard_map(per_device, mesh=mesh, in_specs=in_specs, out_specs=out_specs, check_vma=False)
```

```python
import math

import jax
import jax.numpy as jnp
import numpy as np
from jax import lax
from jax.experimental import pallas as pl
from jax.experimental.pallas import tpu as pltpu
from jax.sharding import PartitionSpec as P

NPTS = 64
ITERS = 6
HALO = 3
LANES = 128
QUARTERS = 4
LIMIT_INNER = 12 * 2**20
LIMIT_FIELD = 24 * 2**20
ROWS = 40

f32 = jnp.float32
bf16 = jnp.bfloat16


def split_bf16(x, parts):
    out = []
    for _ in range(parts):
        out.append(x.astype(bf16))
        x = x - out[-1].astype(f32)
    return out


def gather_kernel(view, volume, out, cells, table, halves):
    wide = jnp.concatenate([volume[...], jnp.zeros((LANES, LANES - 8), jnp.int32)], axis=1)
    cells[...] = jnp.transpose(wide.astype(f32))[:8].astype(jnp.int32)
    for c in range(5):
        rows = [jnp.concatenate([view[c, a, j] for j in range(QUARTERS)], axis=1) for a in range(4)]
        put_halves(halves, c, jnp.concatenate(rows, axis=0))
    table[...] = jnp.zeros((LANES, LANES), f32)
    pitch_of = lax.broadcasted_iota(jnp.int32, (512, LANES), 0)
    row_of = lax.broadcasted_iota(jnp.int32, (64, LANES), 0)

    def pair(n, _):
        slots = [cells[pl.ds(2 * n + k, 1), :] for k in range(2)]
        hot = jnp.concatenate(
            [
                jnp.where(pitch_of == ((cell & 3) << 7) + ((cell & 511) >> 2), 1.0, 0.0).astype(bf16)
                for cell in slots
            ],
            axis=1,
        )
        got = lax.dot_general(
            halves[...], hot, (((1,), (0,)), ((), ())), preferred_element_type=f32
        )
        for k, cell in enumerate(slots):
            here = row_of == (cell >> 9)
            for c in range(5):
                lanes = slice(k * LANES, (k + 1) * LANES)
                both = got[c * 64 : c * 64 + 64, lanes] + got[320 + c * 64 : 384 + c * 64, lanes]
                table[pl.ds(c * 8 + 2 * n + k, 1), :] = jnp.sum(
                    jnp.where(here, both, 0.0), axis=0, keepdims=True
                )
        return 0

    lax.fori_loop(0, 4, pair, 0)
    out[...] = jnp.transpose(table[...])


def gather_samples(view, volume):
    return pl.pallas_call(
        gather_kernel,
        out_shape=jax.ShapeDtypeStruct((LANES, LANES), f32),
        in_specs=[pl.BlockSpec(memory_space=pltpu.VMEM)] * 2,
        out_specs=pl.BlockSpec(memory_space=pltpu.VMEM),
        scratch_shapes=[
            pltpu.VMEM((8, LANES), jnp.int32),
            pltpu.VMEM((LANES, LANES), f32),
            pltpu.VMEM((640, 512), bf16),
        ],
        compiler_params=pltpu.CompilerParams(vmem_limit_bytes=40 * 2**20),
        cost_estimate=pl.CostEstimate(flops=10**9, bytes_accessed=10**6, transcendentals=0),
    )(view, volume)


_levels = np.exp(3.0 * np.arange(NPTS) / (NPTS - 1)) - 1.0
_levels = _levels / (math.exp(3.0) - 1.0)
_spacing = [float(v) for v in _levels[1:] - _levels[:-1]]
_middle = [float(v) for v in 0.5 * (_levels[1:] + _levels[:-1])]


def face_kernel(tiles, surface, height, kelvin, hot, tile_of, live, h, wall):
    target = surface[...]
    lane = lax.broadcasted_iota(jnp.int32, (LANES, LANES), 1)
    low_bits = target & 127
    for k in range(8):
        hot[pl.ds(k * LANES, LANES), :] = jnp.where(lane == low_bits[:, k : k + 1], 1.0, 0.0).astype(bf16)
    wide = jnp.concatenate([target, jnp.zeros((LANES, LANES - 8), jnp.int32)], axis=1)
    by_slot = jnp.transpose(wide.astype(f32))[:8].astype(jnp.int32)
    tile_of[...] = jnp.where(by_slot < 0, -1, by_slot >> 7)
    live[...] = jnp.where(lax.broadcasted_iota(jnp.int32, (8, LANES), 0) < tiles[0], 1.0, 0.0)
    h[...] = height[...]
    wall[...] = kelvin[...]


def face_tables(tiles, surface, height, kelvin):
    tile = jax.ShapeDtypeStruct((8, LANES), f32)
    return pl.pallas_call(
        face_kernel,
        out_shape=(
            jax.ShapeDtypeStruct((8 * LANES, LANES), bf16),
            jax.ShapeDtypeStruct((8, LANES), jnp.int32),
            tile,
            tile,
            tile,
        ),
        in_specs=[pl.BlockSpec(memory_space=pltpu.SMEM)]
        + [pl.BlockSpec(memory_space=pltpu.VMEM)] * 3,
        out_specs=(pl.BlockSpec(memory_space=pltpu.VMEM),) * 5,
        compiler_params=pltpu.CompilerParams(vmem_limit_bytes=40 * 2**20),
        cost_estimate=pl.CostEstimate(flops=10**6, bytes_accessed=10**6, transcendentals=0),
    )(tiles, surface, height, kelvin)


def wall_kernel(received, hot, tile_of, alive, height, kelvin, _mark, out):
    table = jnp.transpose(received[...])
    sub = lax.broadcasted_iota(jnp.int32, (8, LANES), 0)
    here = [sub == tile_of[k : k + 1] for k in range(8)]
    spread = jnp.concatenate(
        [
            jnp.concatenate(
                [jnp.where(here[k], table[c * 8 + k : c * 8 + k + 1], 0.0) for k in range(8)], axis=1
            )
            for c in range(5)
        ],
        axis=0,
    )
    parts = jnp.concatenate(split_bf16(spread, 2), axis=0)
    faces = lax.dot_general(parts, hot[...], (((1,), (0,)), ((), ())), preferred_element_type=f32)
    faces = faces[40:] + faces[:40]
    live = alive[...] > 0.5
    filler = (1.0, 0.4, 0.0, 0.0, 3.0)
    rho, mx, my, mz, energy = (
        jnp.where(live, faces[c * 8 : c * 8 + 8], filler[c]) for c in range(5)
    )
    h = height[...]
    wall = kelvin[...]
    power = mx * mx + my * my + mz * mz
    speed = jnp.sqrt(power) / rho
    temperature = 0.4 * (energy - 0.5 * power / rho) / rho
    tau = 0.002 * speed / h

    def inverse(x):
        return pl.reciprocal(x, approx=True)

    def viscosity(tau):
        friction = jnp.sqrt(tau / rho)
        a = rho * 0.41 * friction * h
        b = friction * rho * h * (-math.log2(math.e) / (0.002 * 17.0))
        return a, b

    def eddy(a, b, j):
        damp = 1.0 - jnp.exp2(b * _middle[j])
        return (a * _middle[j]) * (damp * damp)

    def step(_, tau):
        a, b = viscosity(tau)
        total = [jnp.zeros_like(tau) for _ in range(4)]
        for j in range(NPTS - 1):
            total[j % 4] = total[j % 4] + _spacing[j] * inverse(0.002 + eddy(a, b, j))
        total = (total[0] + total[1]) + (total[2] + total[3])
        return tau * speed / (tau * h * total)

    tau = lax.fori_loop(0, ITERS - 1, step, tau)
    a, b = viscosity(tau)
    total = jnp.zeros_like(tau)
    impedance = jnp.zeros_like(tau)
    work = jnp.zeros_like(tau)
    for j in range(NPTS - 1):
        nu = eddy(a, b, j)
        increment = _spacing[j] * inverse(0.002 + nu)
        total = total + increment
        part = _spacing[j] * inverse(3.5 * (0.002 / 0.72) + (3.5 / 0.9) * nu)
        impedance = impedance + part
        work = work + (total - 0.5 * increment) * part
    scale = tau * h
    rate = (temperature - wall + tau * (scale * h * work)) / (h * impedance)
    tau = tau * speed / (scale * total)
    friction = jnp.where(live, 100.0 * tau / (rho * speed * speed), 0.0)
    heat = jnp.where(live, 100.0 * rate / (rho * 3.5 * speed), 0.0)
    for i in range(8):
        out[0:1, i * LANES : (i + 1) * LANES] = friction[i : i + 1]
        out[1:2, i * LANES : (i + 1) * LANES] = heat[i : i + 1]


def wall_faces(received, tables, mark):
    return pl.pallas_call(
        wall_kernel,
        out_shape=jax.ShapeDtypeStruct((2, 8 * LANES), f32),
        in_specs=[pl.BlockSpec(memory_space=pltpu.VMEM)] * 6 + [pl.BlockSpec(memory_space=pl.ANY)],
        out_specs=pl.BlockSpec(memory_space=pltpu.VMEM),
        compiler_params=pltpu.CompilerParams(vmem_limit_bytes=40 * 2**20),
        cost_estimate=pl.CostEstimate(flops=10**8, bytes_accessed=10**6, transcendentals=10**6),
    )(received, *tables, mark)


def pitch_map(across):
    p = lax.broadcasted_iota(jnp.int32, (512, 512), 1 if across else 0)
    n = lax.broadcasted_iota(jnp.int32, (512, 512), 0 if across else 1)
    return jnp.where(p == 4 * (n & 127) + (n >> 7), 1.0, 0.0).astype(bf16)


def put_halves(halves, c, rows):
    hi, low = split_bf16(rows, 2)
    halves[pl.ds(c * 64, 64), :] = hi
    halves[pl.ds(320 + c * 64, 64), :] = low


def remap(halves, table):
    got = lax.dot_general(halves[...], table, (((1,), (0,)), ((), ())), preferred_element_type=f32)
    return got[:320] + got[320:]


def view_kernel(state, view, first, second, raw, halves, sems):
    copies = [
        [pltpu.make_async_copy(state.at[c, a], raw.at[c, a], sems.at[4 * c + a]) for a in range(4)]
        for c in range(5)
    ]
    for c in range(5):
        for copy in copies[c]:
            copy.start()
    table = pitch_map(False)
    odd = lax.axis_index("stream") % 2
    row_first = (1 - odd) * (16 - HALO)
    row_second = odd * (16 - HALO)
    for c in range(5):
        for copy in copies[c]:
            copy.wait()
        put_halves(halves, c, raw[c].reshape(64, 512))
    x = remap(halves, table)
    for c in range(5):
        for a in range(4):
            for j in range(QUARTERS):
                at = 64 * c + 16 * a
                view[c, a, j] = x[at : at + 16, j * LANES : (j + 1) * LANES]
    for c in range(5):
        for a in range(4):
            for j in range(QUARTERS):
                at = ((c * 4 + a) * QUARTERS + j) * HALO
                first[pl.ds(at, HALO), :] = view[c, a, j, pl.ds(row_first, HALO), :]
                second[pl.ds(at, HALO), :] = view[c, a, j, pl.ds(row_second, HALO), :]


def view_field(state):
    side = jax.ShapeDtypeStruct((5 * 4 * QUARTERS * HALO, LANES), f32)
    return pl.pallas_call(
        view_kernel,
        out_shape=(jax.ShapeDtypeStruct((5, 4, QUARTERS, 16, LANES), f32), side, side),
        in_specs=[pl.BlockSpec(memory_space=pltpu.HBM)],
        out_specs=(pl.BlockSpec(memory_space=pltpu.VMEM),) * 3,
        scratch_shapes=[
            pltpu.VMEM((5, 4, 16, 512), f32),
            pltpu.VMEM((640, 512), bf16),
            pltpu.SemaphoreType.DMA((20,)),
        ],
        compiler_params=pltpu.CompilerParams(vmem_limit_bytes=40 * 2**20),
        cost_estimate=pl.CostEstimate(flops=10**9, bytes_accessed=3 * 10**6, transcendentals=0),
    )(pltpu.with_memory_space_constraint(state, pltpu.HBM))


REACH = ((1, -2, 20, 0), (2, -1, 18, 20), (3, 0, 16, 38))
SIDE = 54


def pack_kernel(view, stream_b, stream_a, _samples, first, second):
    span_odd = lax.axis_index("span") % 2
    stream_odd = lax.axis_index("stream") % 2

    def fill(before, after):
        def body(c, _):
            for out, high in ((first, span_odd == 0), (second, span_odd == 1)):
                for distance, _, count, base in REACH:
                    plane = jnp.where(high, 4 - distance, distance - 1)
                    extra = HALO - distance
                    for j in range(QUARTERS):
                        at = (c * QUARTERS + j) * SIDE + base
                        side = ((c * 4 + plane) * QUARTERS + j) * HALO
                        for i in range(2):
                            out[pl.ds(at + extra + 8 * i, 8), :] = view[c, plane, j, pl.ds(8 * i, 8), :]
                        if extra:
                            out[pl.ds(at, extra), :] = before[pl.ds(side + distance, extra), :]
                            out[pl.ds(at + extra + 16, extra), :] = after[pl.ds(side, extra), :]
            return 0

        lax.fori_loop(0, 5, body, 0)

    @pl.when(stream_odd == 0)
    def _():
        fill(stream_b, stream_a)

    @pl.when(stream_odd == 1)
    def _():
        fill(stream_a, stream_b)


def pack_planes(view, stream_b, stream_a, samples):
    shape = jax.ShapeDtypeStruct((5 * QUARTERS * SIDE, LANES), f32)
    return pl.pallas_call(
        pack_kernel,
        out_shape=(shape, shape),
        in_specs=[pl.BlockSpec(memory_space=pltpu.VMEM)] * 3 + [pl.BlockSpec(memory_space=pl.ANY)],
        out_specs=(pl.BlockSpec(memory_space=pltpu.VMEM),) * 2,
        compiler_params=pltpu.CompilerParams(vmem_limit_bytes=40 * 2**20),
        cost_estimate=pl.CostEstimate(flops=10**6, bytes_accessed=2 * 10**6, transcendentals=0),
    )(view, stream_b, stream_a, samples)


def swap(x, axis, parity):
    spans, streams = lax.axis_size("span"), lax.axis_size("stream")

    def partner(i, n):
        other = i + 1 if i % 2 == parity else i - 1
        return other if 0 <= other < n else None

    pairs = []
    for a in range(spans):
        for b in range(streams):
            if axis == "span":
                other = partner(a, spans)
                there = (a, b ^ 1) if other is None else (other, b)
            else:
                other = partner(b, streams)
                there = (a ^ 1, b) if other is None else (a, other)
            pairs.append((a * streams + b, there[0] * streams + there[1]))
    return lax.ppermute(x, ("span", "stream"), pairs)


NORMAL = ((0, 1, 2, 6), (1, 3, 4, 7), (2, 4, 5, 8))
MIDDLE = (HALO, HALO + 8)


def chunks_from(row):
    return tuple(row - 1 + 8 * i for i in range(3))


def primitive(u):
    rho, m1, m2, m3, energy = u
    inv = pl.reciprocal(rho, approx=True)

    v1, v2, v3 = m1 * inv, m2 * inv, m3 * inv
    t11, t22, t33 = m1 * v1, m2 * v2, m3 * v3
    pressure = 0.4 * energy - 0.2 * (t11 + t22 + t33)
    total = energy + pressure
    square = 1.4 * pressure * inv
    sound = square * lax.rsqrt(square) + 0.04
    return [
        t11 + pressure,
        m1 * v2,
        m1 * v3,
        t22 + pressure,
        m2 * v3,
        t33 + pressure,
        total * v1,
        total * v2,
        total * v3,
        jnp.abs(v1) + sound,
        jnp.abs(v2) + sound,
        jnp.abs(v3) + sound,
    ]


def after(x):
    return jnp.concatenate([x[1:], pltpu.roll(x[:1], LANES - 1, 2)], axis=0)


def before(x):
    return jnp.concatenate([pltpu.roll(x[-1:], 1, 2), x[:-1]], axis=0)


def stage_tools(src, der, gspan, gstream, finish):
    def fill(p, rows):
        for r in rows:
            at = pl.ds(r, 8)
            for n, d in enumerate(primitive([src[c, p, :, at, :] for c in range(5)])):
                der[n, p, :, at, :] = d

    def flux(c, k, p, at):
        return src[1 + k, p, :, at, :] if c == 0 else der[NORMAL[k][c - 1], p, :, at, :]

    def span_faces(p, rows, slot):
        for r in rows:
            at = pl.ds(r, 8)
            coef = jnp.maximum(der[9, p, :, at, :], der[9, p + 1, :, at, :])
            for c in range(5):
                g = (coef - 0.04 if c == 0 else coef) * (src[c, p + 1, :, at, :] - src[c, p, :, at, :])
                gspan[slot, c, :, at, :] = g - (flux(c, 0, p, at) + flux(c, 0, p + 1, at))

    def outputs(p, rows, whole, low_slot, high_slot, faces):
        for i, r in enumerate(rows):
            at, up, down = pl.ds(r, 8), pl.ds(r + 1, 8), pl.ds(r - 1, 8)
            here = der[11, p, :, at, :]
            stream_wave = der[10, p, :, at, :]
            coef_stream = jnp.maximum(stream_wave, der[10, p, :, up, :])
            coef_pitch = jnp.maximum(here, after(here))
            direct = whole and i == 0
            if direct:
                coef_down = jnp.maximum(stream_wave, der[10, p, :, down, :])
            if faces:
                coef_span = jnp.maximum(der[9, p, :, at, :], der[9, p + 1, :, at, :])
            for c in range(5):

                def weigh(coef):
                    return coef - 0.04 if c == 0 else coef

                u = src[c, p, :, at, :]
                if faces:
                    g = weigh(coef_span) * (src[c, p + 1, :, at, :] - u)
                    g = g - (flux(c, 0, p, at) + flux(c, 0, p + 1, at))
                    gspan[high_slot, c, :, at, :] = g
                else:
                    g = gspan[high_slot, c, :, at, :]
                acc = g - gspan[low_slot, c, :, at, :]
                f = flux(c, 1, p, at)
                g = weigh(coef_stream) * (src[c, p, :, up, :] - u) - (f + flux(c, 1, p, up))
                gstream[c, :, pl.ds(r + 8, 8), :] = g
                if direct:
                    low = weigh(coef_down) * (u - src[c, p, :, down, :]) - (f + flux(c, 1, p, down))
                else:
                    low = gstream[c, :, pl.ds(r + 7, 8), :]
                acc = acc + (g - low)
                f = flux(c, 2, p, at)
                h = weigh(coef_pitch) * (after(u) - u) - (f + after(f))
                finish(c, p, r, i, u, acc + (h - before(h)))

    return fill, span_faces, outputs


def clamp_planes(e):
    at = lax.axis_index("span")

    def copy(dst, src):
        for c in range(5):
            for i in range(3):
                e[c, dst, :, pl.ds(8 * i, 8), :] = e[c, src, :, pl.ds(8 * i, 8), :]

    @pl.when(at == 0)
    def _():
        copy(2, 3)

    @pl.when(at == lax.axis_size("span") - 1)
    def _():
        copy(7, 6)


def clamp_rows(e, planes):
    at = lax.axis_index("stream")

    def copy(dst, src):
        for c in range(5):
            for p in planes:
                for q in range(QUARTERS):
                    e[c, p, q, pl.ds(dst, 1), :] = e[c, p, q, pl.ds(src, 1), :]

    @pl.when(at == 0)
    def _():
        copy(2, 3)

    @pl.when(at == lax.axis_size("stream") - 1)
    def _():
        copy(19, 18)


def first_stage(e0, e1):
    def finish(c, p, r, i, u, acc):
        e1[c, p, :, pl.ds(r, 8), :] = u + 0.05 * acc

    return finish


def inner_kernel(view, stream_a, stream_b, e0, e1, der, table, gspan, gstream):
    odd = lax.axis_index("stream") % 2

    def own(c, _):
        for p in range(4):
            for i in range(2):
                e0[c, HALO + p, :, pl.ds(HALO + 8 * i, 8), :] = view[c, p, :, pl.ds(8 * i, 8), :]
        return 0

    lax.fori_loop(0, 5, own, 0)

    def halo_rows(before, after):
        def body(c, _):
            for p in range(4):
                for j in range(QUARTERS):
                    at = ((c * 4 + p) * QUARTERS + j) * HALO
                    e0[c, HALO + p, j, pl.ds(0, HALO), :] = before[pl.ds(at, HALO), :]
                    e0[c, HALO + p, j, pl.ds(HALO + 16, HALO), :] = after[pl.ds(at, HALO), :]
            return 0

        lax.fori_loop(0, 5, body, 0)

    @pl.when(odd == 0)
    def _():
        halo_rows(stream_b, stream_a)

    @pl.when(odd == 1)
    def _():
        halo_rows(stream_a, stream_b)

    clamp_rows(e0, range(3, 7))
    fill, span_faces, outputs = stage_tools(e0, der, gspan, gstream, first_stage(e0, e1))
    wide = chunks_from(1)

    def prims(p, _):
        fill(p, wide)
        return 0

    lax.fori_loop(3, 7, prims, 0)
    span_faces(3, wide, 1)

    def plane(p, _):
        outputs(p, wide, False, 1 - (p & 1), p & 1, True)
        return 0

    lax.fori_loop(4, 6, plane, 0)
    table[...] = pitch_map(True)


def inner_planes(view, stream_a, stream_b):
    block = jax.ShapeDtypeStruct((5, 10, QUARTERS, ROWS, LANES), f32)
    return pl.pallas_call(
        inner_kernel,
        out_shape=(
            block,
            block,
            jax.ShapeDtypeStruct((12, 10, QUARTERS, ROWS, LANES), f32),
            jax.ShapeDtypeStruct((512, 512), bf16),
        ),
        in_specs=[pl.BlockSpec(memory_space=pltpu.VMEM)] * 3,
        out_specs=(pl.BlockSpec(memory_space=pltpu.VMEM),) * 4,
        scratch_shapes=[
            pltpu.VMEM((3, 5, QUARTERS, ROWS, LANES), f32),
            pltpu.VMEM((5, QUARTERS, ROWS + 8, LANES), f32),
        ],
        compiler_params=pltpu.CompilerParams(vmem_limit_bytes=LIMIT_INNER),
        cost_estimate=pl.CostEstimate(flops=10, bytes_accessed=10, transcendentals=0),
    )(view, stream_a, stream_b)


def field_kernel(
    span_a, span_b, table, _e0, _e1, _der, _tile_of, out, mark, e0, e1, der, e2, gspan, gstream, done, result, sems
):
    odd = lax.axis_index("span") % 2

    def halo_planes(before, after):
        def body(c, _):
            for src, high in ((before, False), (after, True)):
                for distance, row, count, base in REACH:
                    plane = 6 + distance if high else HALO - distance
                    for j in range(QUARTERS):
                        at = (c * QUARTERS + j) * SIDE + base
                        for i in range(0, count, 8):
                            n = min(8, count - i)
                            e0[c, plane, j, pl.ds(HALO + row + i, n), :] = src[pl.ds(at + i, n), :]
            return 0

        lax.fori_loop(0, 5, body, 0)

    @pl.when(odd == 0)
    def _():
        halo_planes(span_b, span_a)

    @pl.when(odd == 1)
    def _():
        halo_planes(span_a, span_b)

    clamp_planes(e0)
    clamp_rows(e0, (1, 2, 7, 8))

    fill, span_faces, outputs = stage_tools(e0, der, gspan, gstream, first_stage(e0, e1))
    wide = chunks_from(1)
    fill(0, MIDDLE)
    fill(9, MIDDLE)

    def prims(i, _):
        fill(jnp.where(i < 2, 1 + i, 5 + i), wide)
        return 0

    lax.fori_loop(0, 4, prims, 0)
    span_faces(0, MIDDLE, 0)
    span_faces(1, wide, 1)
    outputs(1, MIDDLE, True, 0, 1, False)
    span_faces(5, wide, 2)

    def plane_one(i, _):
        p = jnp.where(i < 2, 2 + i, 4 + i)
        high = i & 1
        outputs(p, wide, False, jnp.where(i == 2, 2, 1 - high), high, True)
        return 0

    lax.fori_loop(0, 4, plane_one, 0)
    outputs(8, MIDDLE, True, 1, 0, True)

    def finish_two(c, p, r, i, u, acc):
        e2[c, p, :, pl.ds(r, 8), :] = 0.75 * e0[c, p, :, pl.ds(r, 8), :] + (0.25 * u + 0.0125 * acc)

    clamp_planes(e1)
    clamp_rows(e1, range(2, 8))
    fill, span_faces, outputs = stage_tools(e1, der, gspan, gstream, finish_two)
    wide_two = chunks_from(2)
    fill(1, MIDDLE)
    fill(2, wide_two)
    span_faces(1, MIDDLE, 1)
    fill(3, wide_two)
    span_faces(2, wide_two, 0)
    outputs(2, MIDDLE, True, 1, 0, False)

    def plane_two(p, _):
        fill(p + 1, wide_two)
        outputs(p, wide_two, False, 1 - (p & 1), p & 1, True)
        return 0

    lax.fori_loop(3, 7, plane_two, 0)
    fill(8, MIDDLE)
    outputs(7, MIDDLE, True, 0, 1, True)

    def finish_three(c, p, r, i, u, acc):
        new = (1.0 / 3.0) * e0[c, p, :, pl.ds(r, 8), :] + ((2.0 / 3.0) * u + (0.1 / 3.0) * acc)
        for q in range(QUARTERS):
            done[p - HALO, pl.ds(16 * c + 8 * i, 8), q * LANES : (q + 1) * LANES] = new[q]

    copies = []

    def write(p):
        hi, low = split_bf16(done[p], 2)
        got = lax.dot_general(
            jnp.concatenate([hi, low], axis=0),
            table[...],
            (((1,), (0,)), ((), ())),
            preferred_element_type=f32,
        )
        result[p] = (got[:80] + got[80:]).reshape(5, 16, 512)
        copies.append(pltpu.make_async_copy(result.at[p], out.at[:, p], sems.at[p]))
        copies[-1].start()

    clamp_planes(e2)
    clamp_rows(e2, range(3, 7))
    fill, span_faces, outputs = stage_tools(e2, der, gspan, gstream, finish_three)
    wide_three = chunks_from(3)
    fill(2, MIDDLE)
    fill(3, wide_three)
    span_faces(2, MIDDLE, 0)
    for p in range(3, 7):
        fill(p + 1, wide_three if p < 6 else MIDDLE)
        outputs(p, MIDDLE, True, 1 - (p & 1), p & 1, True)
        if p > 3:
            write(p - HALO - 1)
    write(3)
    mark[...] = jnp.zeros((8, LANES), f32)
    for copy in copies:
        copy.wait()


def advance_field(span_a, span_b, inner, tile_of):
    e0, e1, der, table = inner
    vmem = pl.BlockSpec(memory_space=pltpu.VMEM)
    anywhere = pl.BlockSpec(memory_space=pl.ANY)
    out = pl.pallas_call(
        field_kernel,
        out_shape=(
            jax.ShapeDtypeStruct((5, 4, 16, 512), f32),
            jax.ShapeDtypeStruct((8, LANES), f32),
            jax.ShapeDtypeStruct(e0.shape, f32),
            jax.ShapeDtypeStruct(e1.shape, f32),
            jax.ShapeDtypeStruct(der.shape, f32),
        ),
        in_specs=[vmem] * 6 + [anywhere],
        out_specs=(anywhere,) + (vmem,) * 4,
        input_output_aliases={3: 2, 4: 3, 5: 4},
        scratch_shapes=[
            pltpu.VMEM((5, 10, QUARTERS, ROWS, LANES), f32),
            pltpu.VMEM((3, 5, QUARTERS, ROWS, LANES), f32),
            pltpu.VMEM((5, QUARTERS, ROWS + 8, LANES), f32),
            pltpu.VMEM((4, 80, 512), f32),
            pltpu.VMEM((4, 5, 16, 512), f32),
            pltpu.SemaphoreType.DMA((4,)),
        ],
        compiler_params=pltpu.CompilerParams(vmem_limit_bytes=LIMIT_FIELD),
        cost_estimate=pl.CostEstimate(flops=10, bytes_accessed=10, transcendentals=0),
    )(span_a, span_b, table, e0, e1, der, tile_of)
    return out[0], out[1]


def per_device(state, tiles, volume, surface, height, kelvin):
    view, first, second = view_field(state)
    stream_a, stream_b = swap(first, "stream", 0), swap(second, "stream", 1)

    outgoing = gather_samples(view, volume[0])
    received = lax.all_to_all(outgoing, ("span", "stream"), 0, 0, tiled=True)

    first, second = pack_planes(view, stream_b, stream_a, outgoing)
    span_a, span_b = swap(first, "span", 0), swap(second, "span", 1)
    tables = face_tables(tiles, surface[0], height.reshape(8, LANES), kelvin.reshape(8, LANES))
    inner = inner_planes(view, stream_a, stream_b)
    field, mark = advance_field(span_a, span_b, inner, tables[1])
    return field, wall_faces(received, tables, mark)


def solution(mesh):
    in_specs = (
        P(None, "span", "stream", None),
        P(("span", "stream")),
        P(("span", "stream"), None, None),
        P(("span", "stream"), None, None),
        P(("span", "stream")),
        P(("span", "stream")),
    )
    out_specs = (P(None, "span", "stream", None), P(None, ("span", "stream")))
    return jax.shard_map(per_device, mesh=mesh, in_specs=in_specs, out_specs=out_specs, check_vma=False)
```

```python
import math

import jax
import jax.numpy as jnp
import numpy as np
from jax import lax
from jax.experimental import pallas as pl
from jax.experimental.pallas import tpu as pltpu
from jax.sharding import PartitionSpec as P

NPTS = 64
ITERS = 6
HALO = 3
LANES = 128
QUARTERS = 4
LIMIT_INNER = 12 * 2**20
LIMIT_FIELD = 24 * 2**20
ROWS = 40

f32 = jnp.float32
bf16 = jnp.bfloat16


def split_bf16(x, parts):
    out = []
    for _ in range(parts):
        out.append(x.astype(bf16))
        x = x - out[-1].astype(f32)
    return out


def gather_kernel(view, cells, out, table, halves):
    for c in range(5):
        rows = [jnp.concatenate([view[c, a, j] for j in range(QUARTERS)], axis=1) for a in range(4)]
        put_halves(halves, c, jnp.concatenate(rows, axis=0))
    table[...] = jnp.zeros((LANES, LANES), f32)
    pitch_of = lax.broadcasted_iota(jnp.int32, (512, LANES), 0)
    row_of = lax.broadcasted_iota(jnp.int32, (64, LANES), 0)

    def pair(n, _):
        slots = [cells[pl.ds(2 * n + k, 1), :] for k in range(2)]
        hot = jnp.concatenate(
            [
                jnp.where(pitch_of == ((cell & 3) << 7) + ((cell & 511) >> 2), 1.0, 0.0).astype(bf16)
                for cell in slots
            ],
            axis=1,
        )
        got = lax.dot_general(
            halves[...], hot, (((1,), (0,)), ((), ())), preferred_element_type=f32
        )
        for k, cell in enumerate(slots):
            here = row_of == (cell >> 9)
            for c in range(5):
                lanes = slice(k * LANES, (k + 1) * LANES)
                both = got[c * 64 : c * 64 + 64, lanes] + got[320 + c * 64 : 384 + c * 64, lanes]
                table[pl.ds(c * 8 + 2 * n + k, 1), :] = jnp.sum(
                    jnp.where(here, both, 0.0), axis=0, keepdims=True
                )
        return 0

    lax.fori_loop(0, 4, pair, 0)
    out[...] = jnp.transpose(table[...])


def gather_samples(view, volume):
    return pl.pallas_call(
        gather_kernel,
        out_shape=jax.ShapeDtypeStruct((LANES, LANES), f32),
        in_specs=[pl.BlockSpec(memory_space=pltpu.VMEM)] * 2,
        out_specs=pl.BlockSpec(memory_space=pltpu.VMEM),
        scratch_shapes=[
            pltpu.VMEM((LANES, LANES), f32),
            pltpu.VMEM((640, 512), bf16),
        ],
        compiler_params=pltpu.CompilerParams(vmem_limit_bytes=40 * 2**20),
        cost_estimate=pl.CostEstimate(flops=10**9, bytes_accessed=10**6, transcendentals=0),
    )(view, volume)


_levels = np.exp(3.0 * np.arange(NPTS) / (NPTS - 1)) - 1.0
_levels = _levels / (math.exp(3.0) - 1.0)
_spacing = [float(v) for v in _levels[1:] - _levels[:-1]]
_middle = [float(v) for v in 0.5 * (_levels[1:] + _levels[:-1])]


def face_kernel(tiles, surface, height, kelvin, hot, tile_of, live, h, wall):
    by_slot = surface[...]
    tall = jnp.concatenate([by_slot, jnp.zeros((LANES - 8, LANES), jnp.int32)], axis=0)
    low_bits = jnp.transpose(tall.astype(f32)).astype(jnp.int32) & 127
    lane = lax.broadcasted_iota(jnp.int32, (LANES, LANES), 1)
    for k in range(8):
        hot[pl.ds(k * LANES, LANES), :] = jnp.where(lane == low_bits[:, k : k + 1], 1.0, 0.0).astype(bf16)
    tile_of[...] = jnp.where(by_slot < 0, -1, by_slot >> 7)
    live[...] = jnp.where(lax.broadcasted_iota(jnp.int32, (8, LANES), 0) < tiles[0], 1.0, 0.0)
    h[...] = height[...]
    wall[...] = kelvin[...]


def face_tables(tiles, surface, height, kelvin):
    tile = jax.ShapeDtypeStruct((8, LANES), f32)
    return pl.pallas_call(
        face_kernel,
        out_shape=(
            jax.ShapeDtypeStruct((8 * LANES, LANES), bf16),
            jax.ShapeDtypeStruct((8, LANES), jnp.int32),
            tile,
            tile,
            tile,
        ),
        in_specs=[pl.BlockSpec(memory_space=pltpu.SMEM)]
        + [pl.BlockSpec(memory_space=pltpu.VMEM)] * 3,
        out_specs=(pl.BlockSpec(memory_space=pltpu.VMEM),) * 5,
        compiler_params=pltpu.CompilerParams(vmem_limit_bytes=40 * 2**20),
        cost_estimate=pl.CostEstimate(flops=10**6, bytes_accessed=10**6, transcendentals=0),
    )(tiles, surface, height, kelvin)


def wall_kernel(received, hot, tile_of, alive, height, kelvin, _mark, out):
    table = jnp.transpose(received[...])
    sub = lax.broadcasted_iota(jnp.int32, (8, LANES), 0)
    here = [sub == tile_of[k : k + 1] for k in range(8)]
    spread = jnp.concatenate(
        [
            jnp.concatenate(
                [jnp.where(here[k], table[c * 8 + k : c * 8 + k + 1], 0.0) for k in range(8)], axis=1
            )
            for c in range(5)
        ],
        axis=0,
    )
    parts = jnp.concatenate(split_bf16(spread, 2), axis=0)
    faces = lax.dot_general(parts, hot[...], (((1,), (0,)), ((), ())), preferred_element_type=f32)
    faces = faces[40:] + faces[:40]
    live = alive[...] > 0.5
    filler = (1.0, 0.4, 0.0, 0.0, 3.0)
    rho, mx, my, mz, energy = (
        jnp.where(live, faces[c * 8 : c * 8 + 8], filler[c]) for c in range(5)
    )
    h = height[...]
    wall = kelvin[...]
    power = mx * mx + my * my + mz * mz
    speed = jnp.sqrt(power) / rho
    temperature = 0.4 * (energy - 0.5 * power / rho) / rho
    tau = 0.002 * speed / h

    def inverse(x):
        return pl.reciprocal(x, approx=True)

    def viscosity(tau):
        friction = jnp.sqrt(tau / rho)
        a = rho * 0.41 * friction * h
        b = friction * rho * h * (-math.log2(math.e) / (0.002 * 17.0))
        return a, b

    def eddy(a, b, j):
        damp = 1.0 - jnp.exp2(b * _middle[j])
        return (a * _middle[j]) * (damp * damp)

    def step(_, tau):
        a, b = viscosity(tau)
        total = [jnp.zeros_like(tau) for _ in range(4)]
        for j in range(NPTS - 1):
            total[j % 4] = total[j % 4] + _spacing[j] * inverse(0.002 + eddy(a, b, j))
        total = (total[0] + total[1]) + (total[2] + total[3])
        return tau * speed / (tau * h * total)

    tau = lax.fori_loop(0, ITERS - 1, step, tau)
    a, b = viscosity(tau)
    total = jnp.zeros_like(tau)
    impedance = jnp.zeros_like(tau)
    work = jnp.zeros_like(tau)
    for j in range(NPTS - 1):
        nu = eddy(a, b, j)
        increment = _spacing[j] * inverse(0.002 + nu)
        total = total + increment
        part = _spacing[j] * inverse(3.5 * (0.002 / 0.72) + (3.5 / 0.9) * nu)
        impedance = impedance + part
        work = work + (total - 0.5 * increment) * part
    scale = tau * h
    rate = (temperature - wall + tau * (scale * h * work)) / (h * impedance)
    tau = tau * speed / (scale * total)
    friction = jnp.where(live, 100.0 * tau / (rho * speed * speed), 0.0)
    heat = jnp.where(live, 100.0 * rate / (rho * 3.5 * speed), 0.0)
    for i in range(8):
        out[0:1, i * LANES : (i + 1) * LANES] = friction[i : i + 1]
        out[1:2, i * LANES : (i + 1) * LANES] = heat[i : i + 1]


def wall_faces(received, tables, mark):
    return pl.pallas_call(
        wall_kernel,
        out_shape=jax.ShapeDtypeStruct((2, 8 * LANES), f32),
        in_specs=[pl.BlockSpec(memory_space=pltpu.VMEM)] * 6 + [pl.BlockSpec(memory_space=pl.ANY)],
        out_specs=pl.BlockSpec(memory_space=pltpu.VMEM),
        compiler_params=pltpu.CompilerParams(vmem_limit_bytes=40 * 2**20),
        cost_estimate=pl.CostEstimate(flops=10**8, bytes_accessed=10**6, transcendentals=10**6),
    )(received, *tables, mark)


def pitch_map(across):
    p = lax.broadcasted_iota(jnp.int32, (512, 512), 1 if across else 0)
    n = lax.broadcasted_iota(jnp.int32, (512, 512), 0 if across else 1)
    return jnp.where(p == 4 * (n & 127) + (n >> 7), 1.0, 0.0).astype(bf16)


def put_halves(halves, c, rows):
    hi, low = split_bf16(rows, 2)
    halves[pl.ds(c * 64, 64), :] = hi
    halves[pl.ds(320 + c * 64, 64), :] = low


def remap(halves, table):
    got = lax.dot_general(halves[...], table, (((1,), (0,)), ((), ())), preferred_element_type=f32)
    return got[:320] + got[320:]


def view_kernel(state, view, first, second, raw, halves, sems):
    copies = [
        [pltpu.make_async_copy(state.at[c, a], raw.at[c, a], sems.at[4 * c + a]) for a in range(4)]
        for c in range(5)
    ]
    for c in range(5):
        for copy in copies[c]:
            copy.start()
    table = pitch_map(False)
    odd = lax.axis_index("stream") % 2
    row_first = (1 - odd) * (16 - HALO)
    row_second = odd * (16 - HALO)
    for c in range(5):
        for copy in copies[c]:
            copy.wait()
        put_halves(halves, c, raw[c].reshape(64, 512))
    x = remap(halves, table)
    for c in range(5):
        for a in range(4):
            for j in range(QUARTERS):
                at = 64 * c + 16 * a
                view[c, a, j] = x[at : at + 16, j * LANES : (j + 1) * LANES]
    for c in range(5):
        for a in range(4):
            for j in range(QUARTERS):
                at = ((c * 4 + a) * QUARTERS + j) * HALO
                first[pl.ds(at, HALO), :] = view[c, a, j, pl.ds(row_first, HALO), :]
                second[pl.ds(at, HALO), :] = view[c, a, j, pl.ds(row_second, HALO), :]


def view_field(state):
    side = jax.ShapeDtypeStruct((5 * 4 * QUARTERS * HALO, LANES), f32)
    return pl.pallas_call(
        view_kernel,
        out_shape=(jax.ShapeDtypeStruct((5, 4, QUARTERS, 16, LANES), f32), side, side),
        in_specs=[pl.BlockSpec(memory_space=pltpu.HBM)],
        out_specs=(pl.BlockSpec(memory_space=pltpu.VMEM),) * 3,
        scratch_shapes=[
            pltpu.VMEM((5, 4, 16, 512), f32),
            pltpu.VMEM((640, 512), bf16),
            pltpu.SemaphoreType.DMA((20,)),
        ],
        compiler_params=pltpu.CompilerParams(vmem_limit_bytes=40 * 2**20),
        cost_estimate=pl.CostEstimate(flops=10**9, bytes_accessed=3 * 10**6, transcendentals=0),
    )(pltpu.with_memory_space_constraint(state, pltpu.HBM))


REACH = ((1, -2, 20, 0), (2, -1, 18, 20), (3, 0, 16, 38))
SIDE = 54


def pack_kernel(view, stream_b, stream_a, _samples, first, second):
    span_odd = lax.axis_index("span") % 2
    stream_odd = lax.axis_index("stream") % 2

    def fill(before, after):
        def body(c, _):
            for out, high in ((first, span_odd == 0), (second, span_odd == 1)):
                for distance, _, count, base in REACH:
                    plane = jnp.where(high, 4 - distance, distance - 1)
                    extra = HALO - distance
                    for j in range(QUARTERS):
                        at = (c * QUARTERS + j) * SIDE + base
                        side = ((c * 4 + plane) * QUARTERS + j) * HALO
                        for i in range(2):
                            out[pl.ds(at + extra + 8 * i, 8), :] = view[c, plane, j, pl.ds(8 * i, 8), :]
                        if extra:
                            out[pl.ds(at, extra), :] = before[pl.ds(side + distance, extra), :]
                            out[pl.ds(at + extra + 16, extra), :] = after[pl.ds(side, extra), :]
            return 0

        lax.fori_loop(0, 5, body, 0)

    @pl.when(stream_odd == 0)
    def _():
        fill(stream_b, stream_a)

    @pl.when(stream_odd == 1)
    def _():
        fill(stream_a, stream_b)


def pack_planes(view, stream_b, stream_a, samples):
    shape = jax.ShapeDtypeStruct((5 * QUARTERS * SIDE, LANES), f32)
    return pl.pallas_call(
        pack_kernel,
        out_shape=(shape, shape),
        in_specs=[pl.BlockSpec(memory_space=pltpu.VMEM)] * 3 + [pl.BlockSpec(memory_space=pl.ANY)],
        out_specs=(pl.BlockSpec(memory_space=pltpu.VMEM),) * 2,
        compiler_params=pltpu.CompilerParams(vmem_limit_bytes=40 * 2**20),
        cost_estimate=pl.CostEstimate(flops=10**6, bytes_accessed=2 * 10**6, transcendentals=0),
    )(view, stream_b, stream_a, samples)


def swap(x, axis, parity):
    spans, streams = lax.axis_size("span"), lax.axis_size("stream")

    def partner(i, n):
        other = i + 1 if i % 2 == parity else i - 1
        return other if 0 <= other < n else None

    pairs = []
    for a in range(spans):
        for b in range(streams):
            if axis == "span":
                other = partner(a, spans)
                there = (a, b ^ 1) if other is None else (other, b)
            else:
                other = partner(b, streams)
                there = (a ^ 1, b) if other is None else (a, other)
            pairs.append((a * streams + b, there[0] * streams + there[1]))
    return lax.ppermute(x, ("span", "stream"), pairs)


NORMAL = ((0, 1, 2, 6), (1, 3, 4, 7), (2, 4, 5, 8))
MIDDLE = (HALO, HALO + 8)


def chunks_from(row):
    return tuple(row - 1 + 8 * i for i in range(3))


def primitive(u):
    rho, m1, m2, m3, energy = u
    inv = pl.reciprocal(rho, approx=True)

    v1, v2, v3 = m1 * inv, m2 * inv, m3 * inv
    t11, t22, t33 = m1 * v1, m2 * v2, m3 * v3
    pressure = 0.4 * energy - 0.2 * (t11 + t22 + t33)
    total = energy + pressure
    square = 1.4 * pressure * inv
    sound = square * lax.rsqrt(square) + 0.04
    return [
        t11 + pressure,
        m1 * v2,
        m1 * v3,
        t22 + pressure,
        m2 * v3,
        t33 + pressure,
        total * v1,
        total * v2,
        total * v3,
        jnp.abs(v1) + sound,
        jnp.abs(v2) + sound,
        jnp.abs(v3) + sound,
    ]


def after(x):
    return jnp.concatenate([x[1:], pltpu.roll(x[:1], LANES - 1, 2)], axis=0)


def before(x):
    return jnp.concatenate([pltpu.roll(x[-1:], 1, 2), x[:-1]], axis=0)


def stage_tools(src, der, gspan, gstream, finish):
    def fill(p, rows):
        for r in rows:
            at = pl.ds(r, 8)
            for n, d in enumerate(primitive([src[c, p, :, at, :] for c in range(5)])):
                der[n, p, :, at, :] = d

    def flux(c, k, p, at):
        return src[1 + k, p, :, at, :] if c == 0 else der[NORMAL[k][c - 1], p, :, at, :]

    def span_faces(p, rows, slot):
        for r in rows:
            at = pl.ds(r, 8)
            coef = jnp.maximum(der[9, p, :, at, :], der[9, p + 1, :, at, :])
            for c in range(5):
                g = (coef - 0.04 if c == 0 else coef) * (src[c, p + 1, :, at, :] - src[c, p, :, at, :])
                gspan[slot, c, :, at, :] = g - (flux(c, 0, p, at) + flux(c, 0, p + 1, at))

    def outputs(p, rows, whole, low_slot, high_slot, faces):
        for i, r in enumerate(rows):
            at, up, down = pl.ds(r, 8), pl.ds(r + 1, 8), pl.ds(r - 1, 8)
            here = der[11, p, :, at, :]
            stream_wave = der[10, p, :, at, :]
            coef_stream = jnp.maximum(stream_wave, der[10, p, :, up, :])
            coef_pitch = jnp.maximum(here, after(here))
            direct = whole and i == 0
            if direct:
                coef_down = jnp.maximum(stream_wave, der[10, p, :, down, :])
            if faces:
                coef_span = jnp.maximum(der[9, p, :, at, :], der[9, p + 1, :, at, :])
            for c in range(5):

                def weigh(coef):
                    return coef - 0.04 if c == 0 else coef

                u = src[c, p, :, at, :]
                if faces:
                    g = weigh(coef_span) * (src[c, p + 1, :, at, :] - u)
                    g = g - (flux(c, 0, p, at) + flux(c, 0, p + 1, at))
                    gspan[high_slot, c, :, at, :] = g
                else:
                    g = gspan[high_slot, c, :, at, :]
                acc = g - gspan[low_slot, c, :, at, :]
                f = flux(c, 1, p, at)
                g = weigh(coef_stream) * (src[c, p, :, up, :] - u) - (f + flux(c, 1, p, up))
                gstream[c, :, pl.ds(r + 8, 8), :] = g
                if direct:
                    low = weigh(coef_down) * (u - src[c, p, :, down, :]) - (f + flux(c, 1, p, down))
                else:
                    low = gstream[c, :, pl.ds(r + 7, 8), :]
                acc = acc + (g - low)
                f = flux(c, 2, p, at)
                h = weigh(coef_pitch) * (after(u) - u) - (f + after(f))
                finish(c, p, r, i, u, acc + (h - before(h)))

    return fill, span_faces, outputs


def clamp_planes(e):
    at = lax.axis_index("span")

    def copy(dst, src):
        for c in range(5):
            for i in range(3):
                e[c, dst, :, pl.ds(8 * i, 8), :] = e[c, src, :, pl.ds(8 * i, 8), :]

    @pl.when(at == 0)
    def _():
        copy(2, 3)

    @pl.when(at == lax.axis_size("span") - 1)
    def _():
        copy(7, 6)


def clamp_rows(e, planes):
    at = lax.axis_index("stream")

    def copy(dst, src):
        for c in range(5):
            for p in planes:
                for q in range(QUARTERS):
                    e[c, p, q, pl.ds(dst, 1), :] = e[c, p, q, pl.ds(src, 1), :]

    @pl.when(at == 0)
    def _():
        copy(2, 3)

    @pl.when(at == lax.axis_size("stream") - 1)
    def _():
        copy(19, 18)


def first_stage(e0, e1):
    def finish(c, p, r, i, u, acc):
        e1[c, p, :, pl.ds(r, 8), :] = u + 0.05 * acc

    return finish


def inner_kernel(view, stream_a, stream_b, e0, e1, der, table, gspan, gstream):
    odd = lax.axis_index("stream") % 2

    def own(c, _):
        for p in range(4):
            for i in range(2):
                e0[c, HALO + p, :, pl.ds(HALO + 8 * i, 8), :] = view[c, p, :, pl.ds(8 * i, 8), :]
        return 0

    lax.fori_loop(0, 5, own, 0)

    def halo_rows(before, after):
        def body(c, _):
            for p in range(4):
                for j in range(QUARTERS):
                    at = ((c * 4 + p) * QUARTERS + j) * HALO
                    e0[c, HALO + p, j, pl.ds(0, HALO), :] = before[pl.ds(at, HALO), :]
                    e0[c, HALO + p, j, pl.ds(HALO + 16, HALO), :] = after[pl.ds(at, HALO), :]
            return 0

        lax.fori_loop(0, 5, body, 0)

    @pl.when(odd == 0)
    def _():
        halo_rows(stream_b, stream_a)

    @pl.when(odd == 1)
    def _():
        halo_rows(stream_a, stream_b)

    clamp_rows(e0, range(3, 7))
    fill, span_faces, outputs = stage_tools(e0, der, gspan, gstream, first_stage(e0, e1))
    wide = chunks_from(1)

    def prims(p, _):
        fill(p, wide)
        return 0

    lax.fori_loop(3, 7, prims, 0)
    span_faces(3, wide, 1)

    def plane(p, _):
        outputs(p, wide, False, 1 - (p & 1), p & 1, True)
        return 0

    lax.fori_loop(4, 6, plane, 0)
    table[...] = pitch_map(True)


def inner_planes(view, stream_a, stream_b):
    block = jax.ShapeDtypeStruct((5, 10, QUARTERS, ROWS, LANES), f32)
    return pl.pallas_call(
        inner_kernel,
        out_shape=(
            block,
            block,
            jax.ShapeDtypeStruct((12, 10, QUARTERS, ROWS, LANES), f32),
            jax.ShapeDtypeStruct((512, 512), bf16),
        ),
        in_specs=[pl.BlockSpec(memory_space=pltpu.VMEM)] * 3,
        out_specs=(pl.BlockSpec(memory_space=pltpu.VMEM),) * 4,
        scratch_shapes=[
            pltpu.VMEM((3, 5, QUARTERS, ROWS, LANES), f32),
            pltpu.VMEM((5, QUARTERS, ROWS + 8, LANES), f32),
        ],
        compiler_params=pltpu.CompilerParams(vmem_limit_bytes=LIMIT_INNER),
        cost_estimate=pl.CostEstimate(flops=10, bytes_accessed=10, transcendentals=0),
    )(view, stream_a, stream_b)


def field_kernel(
    span_a, span_b, table, _e0, _e1, _der, _tile_of, out, mark, e0, e1, der, e2, gspan, gstream, done, result, sems
):
    odd = lax.axis_index("span") % 2

    def halo_planes(before, after):
        def body(c, _):
            for src, high in ((before, False), (after, True)):
                for distance, row, count, base in REACH:
                    plane = 6 + distance if high else HALO - distance
                    for j in range(QUARTERS):
                        at = (c * QUARTERS + j) * SIDE + base
                        for i in range(0, count, 8):
                            n = min(8, count - i)
                            e0[c, plane, j, pl.ds(HALO + row + i, n), :] = src[pl.ds(at + i, n), :]
            return 0

        lax.fori_loop(0, 5, body, 0)

    @pl.when(odd == 0)
    def _():
        halo_planes(span_b, span_a)

    @pl.when(odd == 1)
    def _():
        halo_planes(span_a, span_b)

    clamp_planes(e0)
    clamp_rows(e0, (1, 2, 7, 8))

    fill, span_faces, outputs = stage_tools(e0, der, gspan, gstream, first_stage(e0, e1))
    wide = chunks_from(1)
    fill(0, MIDDLE)
    fill(9, MIDDLE)

    def prims(i, _):
        fill(jnp.where(i < 2, 1 + i, 5 + i), wide)
        return 0

    lax.fori_loop(0, 4, prims, 0)
    span_faces(0, MIDDLE, 0)
    span_faces(1, wide, 1)
    outputs(1, MIDDLE, True, 0, 1, False)
    span_faces(5, wide, 2)

    def plane_one(i, _):
        p = jnp.where(i < 2, 2 + i, 4 + i)
        high = i & 1
        outputs(p, wide, False, jnp.where(i == 2, 2, 1 - high), high, True)
        return 0

    lax.fori_loop(0, 4, plane_one, 0)
    outputs(8, MIDDLE, True, 1, 0, True)

    def finish_two(c, p, r, i, u, acc):
        e2[c, p, :, pl.ds(r, 8), :] = 0.75 * e0[c, p, :, pl.ds(r, 8), :] + (0.25 * u + 0.0125 * acc)

    clamp_planes(e1)
    clamp_rows(e1, range(2, 8))
    fill, span_faces, outputs = stage_tools(e1, der, gspan, gstream, finish_two)
    wide_two = chunks_from(2)
    fill(1, MIDDLE)
    fill(2, wide_two)
    span_faces(1, MIDDLE, 1)
    fill(3, wide_two)
    span_faces(2, wide_two, 0)
    outputs(2, MIDDLE, True, 1, 0, False)

    def plane_two(p, _):
        fill(p + 1, wide_two)
        outputs(p, wide_two, False, 1 - (p & 1), p & 1, True)
        return 0

    lax.fori_loop(3, 7, plane_two, 0)
    fill(8, MIDDLE)
    outputs(7, MIDDLE, True, 0, 1, True)

    def finish_three(c, p, r, i, u, acc):
        new = (1.0 / 3.0) * e0[c, p, :, pl.ds(r, 8), :] + ((2.0 / 3.0) * u + (0.1 / 3.0) * acc)
        for q in range(QUARTERS):
            done[p - HALO, pl.ds(16 * c + 8 * i, 8), q * LANES : (q + 1) * LANES] = new[q]

    copies = []

    def write(p):
        hi, low = split_bf16(done[p], 2)
        got = lax.dot_general(
            jnp.concatenate([hi, low], axis=0),
            table[...],
            (((1,), (0,)), ((), ())),
            preferred_element_type=f32,
        )
        result[p] = (got[:80] + got[80:]).reshape(5, 16, 512)
        copies.append(pltpu.make_async_copy(result.at[p], out.at[:, p], sems.at[p]))
        copies[-1].start()

    clamp_planes(e2)
    clamp_rows(e2, range(3, 7))
    fill, span_faces, outputs = stage_tools(e2, der, gspan, gstream, finish_three)
    wide_three = chunks_from(3)
    fill(2, MIDDLE)
    fill(3, wide_three)
    span_faces(2, MIDDLE, 0)
    for p in range(3, 7):
        fill(p + 1, wide_three if p < 6 else MIDDLE)
        outputs(p, MIDDLE, True, 1 - (p & 1), p & 1, True)
        if p > 3:
            write(p - HALO - 1)
    write(3)
    mark[...] = jnp.zeros((8, LANES), f32)
    for copy in copies:
        copy.wait()


def advance_field(span_a, span_b, inner, tile_of):
    e0, e1, der, table = inner
    vmem = pl.BlockSpec(memory_space=pltpu.VMEM)
    anywhere = pl.BlockSpec(memory_space=pl.ANY)
    out = pl.pallas_call(
        field_kernel,
        out_shape=(
            jax.ShapeDtypeStruct((5, 4, 16, 512), f32),
            jax.ShapeDtypeStruct((8, LANES), f32),
            jax.ShapeDtypeStruct(e0.shape, f32),
            jax.ShapeDtypeStruct(e1.shape, f32),
            jax.ShapeDtypeStruct(der.shape, f32),
        ),
        in_specs=[vmem] * 6 + [anywhere],
        out_specs=(anywhere,) + (vmem,) * 4,
        input_output_aliases={3: 2, 4: 3, 5: 4},
        scratch_shapes=[
            pltpu.VMEM((5, 10, QUARTERS, ROWS, LANES), f32),
            pltpu.VMEM((3, 5, QUARTERS, ROWS, LANES), f32),
            pltpu.VMEM((5, QUARTERS, ROWS + 8, LANES), f32),
            pltpu.VMEM((4, 80, 512), f32),
            pltpu.VMEM((4, 5, 16, 512), f32),
            pltpu.SemaphoreType.DMA((4,)),
        ],
        compiler_params=pltpu.CompilerParams(vmem_limit_bytes=LIMIT_FIELD),
        cost_estimate=pl.CostEstimate(flops=10, bytes_accessed=10, transcendentals=0),
    )(span_a, span_b, table, e0, e1, der, tile_of)
    return out[0], out[1]


def per_device(state, tiles, volume, surface, height, kelvin):
    view, first, second = view_field(state)
    stream_a, stream_b = swap(first, "stream", 0), swap(second, "stream", 1)

    outgoing = gather_samples(view, volume[0].T)
    received = lax.all_to_all(outgoing, ("span", "stream"), 0, 0, tiled=True)

    first, second = pack_planes(view, stream_b, stream_a, outgoing)
    span_a, span_b = swap(first, "span", 0), swap(second, "span", 1)
    tables = face_tables(tiles, surface[0].T, height.reshape(8, LANES), kelvin.reshape(8, LANES))
    inner = inner_planes(view, stream_a, stream_b)
    field, mark = advance_field(span_a, span_b, inner, tables[1])
    return field, wall_faces(received, tables, mark)


def solution(mesh):
    in_specs = (
        P(None, "span", "stream", None),
        P(("span", "stream")),
        P(("span", "stream"), None, None),
        P(("span", "stream"), None, None),
        P(("span", "stream")),
        P(("span", "stream")),
    )
    out_specs = (P(None, "span", "stream", None), P(None, ("span", "stream")))
    return jax.shard_map(per_device, mesh=mesh, in_specs=in_specs, out_specs=out_specs, check_vma=False)
```

```python
import math

import jax
import jax.numpy as jnp
import numpy as np
from jax import lax
from jax.experimental import pallas as pl
from jax.experimental.pallas import tpu as pltpu
from jax.sharding import PartitionSpec as P

NPTS = 64
ITERS = 6
HALO = 3
LANES = 128
QUARTERS = 4
LIMIT_INNER = 12 * 2**20
LIMIT_FIELD = 24 * 2**20
ROWS = 40

f32 = jnp.float32
bf16 = jnp.bfloat16


def split_bf16(x, parts):
    out = []
    for _ in range(parts):
        out.append(x.astype(bf16))
        x = x - out[-1].astype(f32)
    return out


def gather_kernel(view, cells, out, table, halves):
    for c in range(5):
        rows = [jnp.concatenate([view[c, a, j] for j in range(QUARTERS)], axis=1) for a in range(4)]
        put_halves(halves, c, jnp.concatenate(rows, axis=0))
    table[...] = jnp.zeros((LANES, LANES), f32)
    pitch_of = lax.broadcasted_iota(jnp.int32, (512, LANES), 0)
    row_of = lax.broadcasted_iota(jnp.int32, (64, LANES), 0)

    def pair(n, _):
        slots = [cells[pl.ds(2 * n + k, 1), :] for k in range(2)]
        hot = jnp.concatenate(
            [
                jnp.where(pitch_of == ((cell & 3) << 7) + ((cell & 511) >> 2), 1.0, 0.0).astype(bf16)
                for cell in slots
            ],
            axis=1,
        )
        got = lax.dot_general(
            halves[...], hot, (((1,), (0,)), ((), ())), preferred_element_type=f32
        )
        for k, cell in enumerate(slots):
            here = row_of == (cell >> 9)
            for c in range(5):
                lanes = slice(k * LANES, (k + 1) * LANES)
                both = got[c * 64 : c * 64 + 64, lanes] + got[320 + c * 64 : 384 + c * 64, lanes]
                table[pl.ds(c * 8 + 2 * n + k, 1), :] = jnp.sum(
                    jnp.where(here, both, 0.0), axis=0, keepdims=True
                )
        return 0

    lax.fori_loop(0, 4, pair, 0)
    out[...] = jnp.transpose(table[...])


def gather_samples(view, volume):
    return pl.pallas_call(
        gather_kernel,
        out_shape=jax.ShapeDtypeStruct((LANES, LANES), f32),
        in_specs=[pl.BlockSpec(memory_space=pltpu.VMEM)] * 2,
        out_specs=pl.BlockSpec(memory_space=pltpu.VMEM),
        scratch_shapes=[
            pltpu.VMEM((LANES, LANES), f32),
            pltpu.VMEM((640, 512), bf16),
        ],
        compiler_params=pltpu.CompilerParams(vmem_limit_bytes=40 * 2**20),
        cost_estimate=pl.CostEstimate(flops=10**9, bytes_accessed=10**6, transcendentals=0),
    )(view, volume)


_levels = np.exp(3.0 * np.arange(NPTS) / (NPTS - 1)) - 1.0
_levels = _levels / (math.exp(3.0) - 1.0)
_spacing = [float(v) for v in _levels[1:] - _levels[:-1]]
_middle = [float(v) for v in 0.5 * (_levels[1:] + _levels[:-1])]


def face_kernel(tiles, surface, height, kelvin, hot, tile_of, live, h, wall):
    by_slot = surface[...]
    tall = jnp.concatenate([by_slot, jnp.zeros((LANES - 8, LANES), jnp.int32)], axis=0)
    low_bits = jnp.transpose(tall.astype(f32)).astype(jnp.int32) & 127
    lane = lax.broadcasted_iota(jnp.int32, (LANES, LANES), 1)
    for k in range(8):
        hot[pl.ds(k * LANES, LANES), :] = jnp.where(lane == low_bits[:, k : k + 1], 1.0, 0.0).astype(bf16)
    tile_of[...] = jnp.where(by_slot < 0, -1, by_slot >> 7)
    live[...] = jnp.where(lax.broadcasted_iota(jnp.int32, (8, LANES), 0) < tiles[0], 1.0, 0.0)
    h[...] = height[...]
    wall[...] = kelvin[...]


def face_tables(tiles, surface, height, kelvin):
    tile = jax.ShapeDtypeStruct((8, LANES), f32)
    return pl.pallas_call(
        face_kernel,
        out_shape=(
            jax.ShapeDtypeStruct((8 * LANES, LANES), bf16),
            jax.ShapeDtypeStruct((8, LANES), jnp.int32),
            tile,
            tile,
            tile,
        ),
        in_specs=[pl.BlockSpec(memory_space=pltpu.SMEM)]
        + [pl.BlockSpec(memory_space=pltpu.VMEM)] * 3,
        out_specs=(pl.BlockSpec(memory_space=pltpu.VMEM),) * 5,
        compiler_params=pltpu.CompilerParams(vmem_limit_bytes=40 * 2**20),
        cost_estimate=pl.CostEstimate(flops=10**6, bytes_accessed=10**6, transcendentals=0),
    )(tiles, surface, height, kelvin)


def wall_kernel(received, hot, tile_of, alive, height, kelvin, _mark, out):
    table = jnp.transpose(received[...])
    sub = lax.broadcasted_iota(jnp.int32, (8, LANES), 0)
    here = [sub == tile_of[k : k + 1] for k in range(8)]
    spread = jnp.concatenate(
        [
            jnp.concatenate(
                [jnp.where(here[k], table[c * 8 + k : c * 8 + k + 1], 0.0) for k in range(8)], axis=1
            )
            for c in range(5)
        ],
        axis=0,
    )
    parts = jnp.concatenate(split_bf16(spread, 2), axis=0)
    faces = lax.dot_general(parts, hot[...], (((1,), (0,)), ((), ())), preferred_element_type=f32)
    faces = faces[40:] + faces[:40]
    live = alive[...] > 0.5
    filler = (1.0, 0.4, 0.0, 0.0, 3.0)
    rho, mx, my, mz, energy = (
        jnp.where(live, faces[c * 8 : c * 8 + 8], filler[c]) for c in range(5)
    )
    h = height[...]
    wall = kelvin[...]
    power = mx * mx + my * my + mz * mz
    speed = jnp.sqrt(power) / rho
    temperature = 0.4 * (energy - 0.5 * power / rho) / rho
    tau = 0.002 * speed / h

    def inverse(x):
        return pl.reciprocal(x, approx=True)

    def viscosity(tau):
        friction = jnp.sqrt(tau / rho)
        a = rho * 0.41 * friction * h
        b = friction * rho * h * (-math.log2(math.e) / (0.002 * 17.0))
        return a, b

    def eddy(a, b, j):
        damp = 1.0 - jnp.exp2(b * _middle[j])
        return a * (damp * damp)

    def step(_, tau):
        a, b = viscosity(tau)
        total = [jnp.zeros_like(tau) for _ in range(4)]
        for j in range(NPTS - 1):
            total[j % 4] = total[j % 4] + (_spacing[j] / _middle[j]) * inverse(0.002 / _middle[j] + eddy(a, b, j))
        total = (total[0] + total[1]) + (total[2] + total[3])
        return tau * speed / (tau * h * total)

    tau = lax.fori_loop(0, ITERS - 1, step, tau)
    a, b = viscosity(tau)
    total = jnp.zeros_like(tau)
    impedance = jnp.zeros_like(tau)
    work = jnp.zeros_like(tau)
    for j in range(NPTS - 1):
        nu = eddy(a, b, j)
        increment = (_spacing[j] / _middle[j]) * inverse(0.002 / _middle[j] + nu)
        total = total + increment
        part = (_spacing[j] / _middle[j] / (3.5 / 0.9)) * inverse((0.9 / 0.72) * 0.002 / _middle[j] + nu)
        impedance = impedance + part
        work = work + (total - 0.5 * increment) * part
    scale = tau * h
    rate = (temperature - wall + tau * (scale * h * work)) / (h * impedance)
    tau = tau * speed / (scale * total)
    friction = jnp.where(live, 100.0 * tau / (rho * speed * speed), 0.0)
    heat = jnp.where(live, 100.0 * rate / (rho * 3.5 * speed), 0.0)
    for i in range(8):
        out[0:1, i * LANES : (i + 1) * LANES] = friction[i : i + 1]
        out[1:2, i * LANES : (i + 1) * LANES] = heat[i : i + 1]


def wall_faces(received, tables, mark):
    return pl.pallas_call(
        wall_kernel,
        out_shape=jax.ShapeDtypeStruct((2, 8 * LANES), f32),
        in_specs=[pl.BlockSpec(memory_space=pltpu.VMEM)] * 6 + [pl.BlockSpec(memory_space=pl.ANY)],
        out_specs=pl.BlockSpec(memory_space=pltpu.VMEM),
        compiler_params=pltpu.CompilerParams(vmem_limit_bytes=40 * 2**20),
        cost_estimate=pl.CostEstimate(flops=10**8, bytes_accessed=10**6, transcendentals=10**6),
    )(received, *tables, mark)


def pitch_map(across):
    p = lax.broadcasted_iota(jnp.int32, (512, 512), 1 if across else 0)
    n = lax.broadcasted_iota(jnp.int32, (512, 512), 0 if across else 1)
    return jnp.where(p == 4 * (n & 127) + (n >> 7), 1.0, 0.0).astype(bf16)


def put_halves(halves, c, rows):
    hi, low = split_bf16(rows, 2)
    halves[pl.ds(c * 64, 64), :] = hi
    halves[pl.ds(320 + c * 64, 64), :] = low


def remap(halves, table):
    got = lax.dot_general(halves[...], table, (((1,), (0,)), ((), ())), preferred_element_type=f32)
    return got[:320] + got[320:]


def view_kernel(state, view, first, second, halves):
    table = pitch_map(False)
    odd = lax.axis_index("stream") % 2
    row_first = (1 - odd) * (16 - HALO)
    row_second = odd * (16 - HALO)
    for c in range(5):
        put_halves(halves, c, state[c].reshape(64, 512))
    x = remap(halves, table)
    for c in range(5):
        for a in range(4):
            for j in range(QUARTERS):
                at = 64 * c + 16 * a
                view[c, a, j] = x[at : at + 16, j * LANES : (j + 1) * LANES]
    for c in range(5):
        for a in range(4):
            for j in range(QUARTERS):
                at = ((c * 4 + a) * QUARTERS + j) * HALO
                first[pl.ds(at, HALO), :] = view[c, a, j, pl.ds(row_first, HALO), :]
                second[pl.ds(at, HALO), :] = view[c, a, j, pl.ds(row_second, HALO), :]


def view_field(state):
    side = jax.ShapeDtypeStruct((5 * 4 * QUARTERS * HALO, LANES), f32)
    return pl.pallas_call(
        view_kernel,
        out_shape=(jax.ShapeDtypeStruct((5, 4, QUARTERS, 16, LANES), f32), side, side),
        in_specs=[pl.BlockSpec(memory_space=pltpu.VMEM)],
        out_specs=(pl.BlockSpec(memory_space=pltpu.VMEM),) * 3,
        scratch_shapes=[
            pltpu.VMEM((640, 512), bf16),
        ],
        compiler_params=pltpu.CompilerParams(vmem_limit_bytes=40 * 2**20),
        cost_estimate=pl.CostEstimate(flops=10**9, bytes_accessed=3 * 10**6, transcendentals=0),
    )(state)


REACH = ((1, -2, 20, 0), (2, -1, 18, 20), (3, 0, 16, 38))
SIDE = 54


def pack_kernel(view, stream_b, stream_a, _samples, first, second):
    span_odd = lax.axis_index("span") % 2
    stream_odd = lax.axis_index("stream") % 2

    def fill(before, after):
        def body(c, _):
            for out, high in ((first, span_odd == 0), (second, span_odd == 1)):
                for distance, _, count, base in REACH:
                    plane = jnp.where(high, 4 - distance, distance - 1)
                    extra = HALO - distance
                    for j in range(QUARTERS):
                        at = (c * QUARTERS + j) * SIDE + base
                        side = ((c * 4 + plane) * QUARTERS + j) * HALO
                        for i in range(2):
                            out[pl.ds(at + extra + 8 * i, 8), :] = view[c, plane, j, pl.ds(8 * i, 8), :]
                        if extra:
                            out[pl.ds(at, extra), :] = before[pl.ds(side + distance, extra), :]
                            out[pl.ds(at + extra + 16, extra), :] = after[pl.ds(side, extra), :]
            return 0

        lax.fori_loop(0, 5, body, 0)

    @pl.when(stream_odd == 0)
    def _():
        fill(stream_b, stream_a)

    @pl.when(stream_odd == 1)
    def _():
        fill(stream_a, stream_b)


def pack_planes(view, stream_b, stream_a, samples):
    shape = jax.ShapeDtypeStruct((5 * QUARTERS * SIDE, LANES), f32)
    return pl.pallas_call(
        pack_kernel,
        out_shape=(shape, shape),
        in_specs=[pl.BlockSpec(memory_space=pltpu.VMEM)] * 3 + [pl.BlockSpec(memory_space=pl.ANY)],
        out_specs=(pl.BlockSpec(memory_space=pltpu.VMEM),) * 2,
        compiler_params=pltpu.CompilerParams(vmem_limit_bytes=40 * 2**20),
        cost_estimate=pl.CostEstimate(flops=10**6, bytes_accessed=2 * 10**6, transcendentals=0),
    )(view, stream_b, stream_a, samples)


def swap(x, axis, parity):
    spans, streams = lax.axis_size("span"), lax.axis_size("stream")

    def partner(i, n):
        other = i + 1 if i % 2 == parity else i - 1
        return other if 0 <= other < n else None

    pairs = []
    for a in range(spans):
        for b in range(streams):
            if axis == "span":
                other = partner(a, spans)
                there = (a, b ^ 1) if other is None else (other, b)
            else:
                other = partner(b, streams)
                there = (a ^ 1, b) if other is None else (a, other)
            pairs.append((a * streams + b, there[0] * streams + there[1]))
    return lax.ppermute(x, ("span", "stream"), pairs)


NORMAL = ((0, 1, 2, 6), (1, 3, 4, 7), (2, 4, 5, 8))
MIDDLE = (HALO, HALO + 8)


def chunks_from(row):
    return tuple(row - 1 + 8 * i for i in range(3))


def primitive(u):
    rho, m1, m2, m3, energy = u
    inv = pl.reciprocal(rho, approx=True)

    v1, v2, v3 = m1 * inv, m2 * inv, m3 * inv
    t11, t22, t33 = m1 * v1, m2 * v2, m3 * v3
    pressure = 0.4 * energy - 0.2 * (t11 + t22 + t33)
    total = energy + pressure
    square = 1.4 * pressure * inv
    sound = square * lax.rsqrt(square) + 0.04
    return [
        t11 + pressure,
        m1 * v2,
        m1 * v3,
        t22 + pressure,
        m2 * v3,
        t33 + pressure,
        total * v1,
        total * v2,
        total * v3,
        jnp.abs(v1) + sound,
        jnp.abs(v2) + sound,
        jnp.abs(v3) + sound,
    ]


def after(x):
    return jnp.concatenate([x[1:], pltpu.roll(x[:1], LANES - 1, 2)], axis=0)


def before(x):
    return jnp.concatenate([pltpu.roll(x[-1:], 1, 2), x[:-1]], axis=0)


def stage_tools(src, der, gspan, gstream, finish):
    def fill(p, rows):
        for r in rows:
            at = pl.ds(r, 8)
            for n, d in enumerate(primitive([src[c, p, :, at, :] for c in range(5)])):
                der[n, p, :, at, :] = d

    def flux(c, k, p, at):
        return src[1 + k, p, :, at, :] if c == 0 else der[NORMAL[k][c - 1], p, :, at, :]

    def span_faces(p, rows, slot):
        for r in rows:
            at = pl.ds(r, 8)
            coef = jnp.maximum(der[9, p, :, at, :], der[9, p + 1, :, at, :])
            for c in range(5):
                g = (coef - 0.04 if c == 0 else coef) * (src[c, p + 1, :, at, :] - src[c, p, :, at, :])
                gspan[slot, c, :, at, :] = g - (flux(c, 0, p, at) + flux(c, 0, p + 1, at))

    def outputs(p, rows, whole, low_slot, high_slot, faces):
        for i, r in enumerate(rows):
            at, up, down = pl.ds(r, 8), pl.ds(r + 1, 8), pl.ds(r - 1, 8)
            here = der[11, p, :, at, :]
            stream_wave = der[10, p, :, at, :]
            coef_stream = jnp.maximum(stream_wave, der[10, p, :, up, :])
            coef_pitch = jnp.maximum(here, after(here))
            direct = whole and i == 0
            if direct:
                coef_down = jnp.maximum(stream_wave, der[10, p, :, down, :])
            if faces:
                coef_span = jnp.maximum(der[9, p, :, at, :], der[9, p + 1, :, at, :])
            for c in range(5):

                def weigh(coef):
                    return coef - 0.04 if c == 0 else coef

                u = src[c, p, :, at, :]
                if faces:
                    g = weigh(coef_span) * (src[c, p + 1, :, at, :] - u)
                    g = g - (flux(c, 0, p, at) + flux(c, 0, p + 1, at))
                    gspan[high_slot, c, :, at, :] = g
                else:
                    g = gspan[high_slot, c, :, at, :]
                acc = g - gspan[low_slot, c, :, at, :]
                f = flux(c, 1, p, at)
                g = weigh(coef_stream) * (src[c, p, :, up, :] - u) - (f + flux(c, 1, p, up))
                gstream[c, :, pl.ds(r + 8, 8), :] = g
                if direct:
                    low = weigh(coef_down) * (u - src[c, p, :, down, :]) - (f + flux(c, 1, p, down))
                else:
                    low = gstream[c, :, pl.ds(r + 7, 8), :]
                acc = acc + (g - low)
                f = flux(c, 2, p, at)
                h = weigh(coef_pitch) * (after(u) - u) - (f + after(f))
                finish(c, p, r, i, u, acc + (h - before(h)))

    return fill, span_faces, outputs


def clamp_planes(e):
    at = lax.axis_index("span")

    def copy(dst, src):
        for c in range(5):
            for i in range(3):
                e[c, dst, :, pl.ds(8 * i, 8), :] = e[c, src, :, pl.ds(8 * i, 8), :]

    @pl.when(at == 0)
    def _():
        copy(2, 3)

    @pl.when(at == lax.axis_size("span") - 1)
    def _():
        copy(7, 6)


def clamp_rows(e, planes):
    at = lax.axis_index("stream")

    def copy(dst, src):
        for c in range(5):
            for p in planes:
                for q in range(QUARTERS):
                    e[c, p, q, pl.ds(dst, 1), :] = e[c, p, q, pl.ds(src, 1), :]

    @pl.when(at == 0)
    def _():
        copy(2, 3)

    @pl.when(at == lax.axis_size("stream") - 1)
    def _():
        copy(19, 18)


def first_stage(e0, e1):
    def finish(c, p, r, i, u, acc):
        e1[c, p, :, pl.ds(r, 8), :] = u + 0.05 * acc

    return finish


def inner_kernel(view, stream_a, stream_b, e0, e1, der, table, gspan, gstream):
    odd = lax.axis_index("stream") % 2

    def own(c, _):
        for p in range(4):
            for i in range(2):
                e0[c, HALO + p, :, pl.ds(HALO + 8 * i, 8), :] = view[c, p, :, pl.ds(8 * i, 8), :]
        return 0

    lax.fori_loop(0, 5, own, 0)

    def halo_rows(before, after):
        def body(c, _):
            for p in range(4):
                for j in range(QUARTERS):
                    at = ((c * 4 + p) * QUARTERS + j) * HALO
                    e0[c, HALO + p, j, pl.ds(0, HALO), :] = before[pl.ds(at, HALO), :]
                    e0[c, HALO + p, j, pl.ds(HALO + 16, HALO), :] = after[pl.ds(at, HALO), :]
            return 0

        lax.fori_loop(0, 5, body, 0)

    @pl.when(odd == 0)
    def _():
        halo_rows(stream_b, stream_a)

    @pl.when(odd == 1)
    def _():
        halo_rows(stream_a, stream_b)

    clamp_rows(e0, range(3, 7))
    fill, span_faces, outputs = stage_tools(e0, der, gspan, gstream, first_stage(e0, e1))
    wide = chunks_from(1)

    def prims(p, _):
        fill(p, wide)
        return 0

    lax.fori_loop(3, 7, prims, 0)
    span_faces(3, wide, 1)

    def plane(p, _):
        outputs(p, wide, False, 1 - (p & 1), p & 1, True)
        return 0

    lax.fori_loop(4, 6, plane, 0)
    table[...] = pitch_map(True)


def inner_planes(view, stream_a, stream_b):
    block = jax.ShapeDtypeStruct((5, 10, QUARTERS, ROWS, LANES), f32)
    return pl.pallas_call(
        inner_kernel,
        out_shape=(
            block,
            block,
            jax.ShapeDtypeStruct((12, 10, QUARTERS, ROWS, LANES), f32),
            jax.ShapeDtypeStruct((512, 512), bf16),
        ),
        in_specs=[pl.BlockSpec(memory_space=pltpu.VMEM)] * 3,
        out_specs=(pl.BlockSpec(memory_space=pltpu.VMEM),) * 4,
        scratch_shapes=[
            pltpu.VMEM((3, 5, QUARTERS, ROWS, LANES), f32),
            pltpu.VMEM((5, QUARTERS, ROWS + 8, LANES), f32),
        ],
        compiler_params=pltpu.CompilerParams(vmem_limit_bytes=LIMIT_INNER),
        cost_estimate=pl.CostEstimate(flops=10, bytes_accessed=10, transcendentals=0),
    )(view, stream_a, stream_b)


def field_kernel(
    span_a, span_b, table, _e0, _e1, _der, _tile_of, out, mark, e0, e1, der, e2, gspan, gstream, done, result, sems
):
    odd = lax.axis_index("span") % 2

    def halo_planes(before, after):
        def body(c, _):
            for src, high in ((before, False), (after, True)):
                for distance, row, count, base in REACH:
                    plane = 6 + distance if high else HALO - distance
                    for j in range(QUARTERS):
                        at = (c * QUARTERS + j) * SIDE + base
                        for i in range(0, count, 8):
                            n = min(8, count - i)
                            e0[c, plane, j, pl.ds(HALO + row + i, n), :] = src[pl.ds(at + i, n), :]
            return 0

        lax.fori_loop(0, 5, body, 0)

    @pl.when(odd == 0)
    def _():
        halo_planes(span_b, span_a)

    @pl.when(odd == 1)
    def _():
        halo_planes(span_a, span_b)

    clamp_planes(e0)
    clamp_rows(e0, (1, 2, 7, 8))

    fill, span_faces, outputs = stage_tools(e0, der, gspan, gstream, first_stage(e0, e1))
    wide = chunks_from(1)
    fill(0, MIDDLE)
    fill(9, MIDDLE)

    def prims(i, _):
        fill(jnp.where(i < 2, 1 + i, 5 + i), wide)
        return 0

    lax.fori_loop(0, 4, prims, 0)
    span_faces(0, MIDDLE, 0)
    span_faces(1, wide, 1)
    outputs(1, MIDDLE, True, 0, 1, False)
    span_faces(5, wide, 2)

    def plane_one(i, _):
        p = jnp.where(i < 2, 2 + i, 4 + i)
        high = i & 1
        outputs(p, wide, False, jnp.where(i == 2, 2, 1 - high), high, True)
        return 0

    lax.fori_loop(0, 4, plane_one, 0)
    outputs(8, MIDDLE, True, 1, 0, True)

    def finish_two(c, p, r, i, u, acc):
        e2[c, p, :, pl.ds(r, 8), :] = 0.75 * e0[c, p, :, pl.ds(r, 8), :] + (0.25 * u + 0.0125 * acc)

    clamp_planes(e1)
    clamp_rows(e1, range(2, 8))
    fill, span_faces, outputs = stage_tools(e1, der, gspan, gstream, finish_two)
    wide_two = chunks_from(2)
    fill(1, MIDDLE)
    fill(2, wide_two)
    span_faces(1, MIDDLE, 1)
    fill(3, wide_two)
    span_faces(2, wide_two, 0)
    outputs(2, MIDDLE, True, 1, 0, False)

    def plane_two(p, _):
        fill(p + 1, wide_two)
        outputs(p, wide_two, False, 1 - (p & 1), p & 1, True)
        return 0

    lax.fori_loop(3, 7, plane_two, 0)
    fill(8, MIDDLE)
    outputs(7, MIDDLE, True, 0, 1, True)

    def finish_three(c, p, r, i, u, acc):
        new = (1.0 / 3.0) * e0[c, p, :, pl.ds(r, 8), :] + ((2.0 / 3.0) * u + (0.1 / 3.0) * acc)
        for q in range(QUARTERS):
            done[p - HALO, pl.ds(16 * c + 8 * i, 8), q * LANES : (q + 1) * LANES] = new[q]

    copies = []

    def write(p):
        hi, low = split_bf16(done[p], 2)
        got = lax.dot_general(
            jnp.concatenate([hi, low], axis=0),
            table[...],
            (((1,), (0,)), ((), ())),
            preferred_element_type=f32,
        )
        result[p] = (got[:80] + got[80:]).reshape(5, 16, 512)
        copies.append(pltpu.make_async_copy(result.at[p], out.at[:, p], sems.at[p]))
        copies[-1].start()

    clamp_planes(e2)
    clamp_rows(e2, range(3, 7))
    fill, span_faces, outputs = stage_tools(e2, der, gspan, gstream, finish_three)
    wide_three = chunks_from(3)
    fill(2, MIDDLE)
    fill(3, wide_three)
    span_faces(2, MIDDLE, 0)
    for p in range(3, 7):
        fill(p + 1, wide_three if p < 6 else MIDDLE)
        outputs(p, MIDDLE, True, 1 - (p & 1), p & 1, True)
        if p > 3:
            write(p - HALO - 1)
    write(3)
    mark[...] = jnp.zeros((8, LANES), f32)
    for copy in copies:
        copy.wait()


def advance_field(span_a, span_b, inner, tile_of):
    e0, e1, der, table = inner
    vmem = pl.BlockSpec(memory_space=pltpu.VMEM)
    anywhere = pl.BlockSpec(memory_space=pl.ANY)
    out = pl.pallas_call(
        field_kernel,
        out_shape=(
            jax.ShapeDtypeStruct((5, 4, 16, 512), f32),
            jax.ShapeDtypeStruct((8, LANES), f32),
            jax.ShapeDtypeStruct(e0.shape, f32),
            jax.ShapeDtypeStruct(e1.shape, f32),
            jax.ShapeDtypeStruct(der.shape, f32),
        ),
        in_specs=[vmem] * 6 + [anywhere],
        out_specs=(anywhere,) + (vmem,) * 4,
        input_output_aliases={3: 2, 4: 3, 5: 4},
        scratch_shapes=[
            pltpu.VMEM((5, 10, QUARTERS, ROWS, LANES), f32),
            pltpu.VMEM((3, 5, QUARTERS, ROWS, LANES), f32),
            pltpu.VMEM((5, QUARTERS, ROWS + 8, LANES), f32),
            pltpu.VMEM((4, 80, 512), f32),
            pltpu.VMEM((4, 5, 16, 512), f32),
            pltpu.SemaphoreType.DMA((4,)),
        ],
        compiler_params=pltpu.CompilerParams(vmem_limit_bytes=LIMIT_FIELD),
        cost_estimate=pl.CostEstimate(flops=10, bytes_accessed=10, transcendentals=0),
    )(span_a, span_b, table, e0, e1, der, tile_of)
    return out[0], out[1]


def per_device(state, tiles, volume, surface, height, kelvin):
    view, first, second = view_field(state)
    stream_a, stream_b = swap(first, "stream", 0), swap(second, "stream", 1)

    outgoing = gather_samples(view, volume[0].T)
    received = lax.all_to_all(outgoing, ("span", "stream"), 0, 0, tiled=True)

    first, second = pack_planes(view, stream_b, stream_a, outgoing)
    span_a, span_b = swap(first, "span", 0), swap(second, "span", 1)
    tables = face_tables(tiles, surface[0].T, height.reshape(8, LANES), kelvin.reshape(8, LANES))
    inner = inner_planes(view, stream_a, stream_b)
    field, mark = advance_field(span_a, span_b, inner, tables[1])
    return field, wall_faces(received, tables, mark)


def solution(mesh):
    in_specs = (
        P(None, "span", "stream", None),
        P(("span", "stream")),
        P(("span", "stream"), None, None),
        P(("span", "stream"), None, None),
        P(("span", "stream")),
        P(("span", "stream")),
    )
    out_specs = (P(None, "span", "stream", None), P(None, ("span", "stream")))
    return jax.shard_map(per_device, mesh=mesh, in_specs=in_specs, out_specs=out_specs, check_vma=False)
```

```python
import math

import jax
import jax.numpy as jnp
import numpy as np
from jax import lax
from jax.experimental import pallas as pl
from jax.experimental.pallas import tpu as pltpu
from jax.sharding import PartitionSpec as P

NPTS = 64
ITERS = 6
HALO = 3
LANES = 128
QUARTERS = 4
LIMIT_INNER = 12 * 2**20
LIMIT_FIELD = 24 * 2**20
ROWS = 40

f32 = jnp.float32
bf16 = jnp.bfloat16


def split_bf16(x, parts):
    out = []
    for _ in range(parts):
        out.append(x.astype(bf16))
        x = x - out[-1].astype(f32)
    return out


def gather_kernel(view, cells, out, table, halves):
    for c in range(5):
        rows = [jnp.concatenate([view[c, a, j] for j in range(QUARTERS)], axis=1) for a in range(4)]
        put_halves(halves, c, jnp.concatenate(rows, axis=0))
    table[...] = jnp.zeros((LANES, LANES), f32)
    pitch_of = lax.broadcasted_iota(jnp.int32, (512, LANES), 0)
    row_of = lax.broadcasted_iota(jnp.int32, (64, LANES), 0)

    def pair(n, _):
        slots = [cells[pl.ds(2 * n + k, 1), :] for k in range(2)]
        hot = jnp.concatenate(
            [
                jnp.where(pitch_of == ((cell & 3) << 7) + ((cell & 511) >> 2), 1.0, 0.0).astype(bf16)
                for cell in slots
            ],
            axis=1,
        )
        got = lax.dot_general(
            halves[...], hot, (((1,), (0,)), ((), ())), preferred_element_type=f32
        )
        for k, cell in enumerate(slots):
            here = row_of == (cell >> 9)
            for c in range(5):
                lanes = slice(k * LANES, (k + 1) * LANES)
                both = got[c * 64 : c * 64 + 64, lanes] + got[320 + c * 64 : 384 + c * 64, lanes]
                table[pl.ds(c * 8 + 2 * n + k, 1), :] = jnp.sum(
                    jnp.where(here, both, 0.0), axis=0, keepdims=True
                )
        return 0

    lax.fori_loop(0, 4, pair, 0)
    out[...] = jnp.transpose(table[...])


def gather_samples(view, volume):
    return pl.pallas_call(
        gather_kernel,
        out_shape=jax.ShapeDtypeStruct((LANES, LANES), f32),
        in_specs=[pl.BlockSpec(memory_space=pltpu.VMEM)] * 2,
        out_specs=pl.BlockSpec(memory_space=pltpu.VMEM),
        scratch_shapes=[
            pltpu.VMEM((LANES, LANES), f32),
            pltpu.VMEM((640, 512), bf16),
        ],
        compiler_params=pltpu.CompilerParams(vmem_limit_bytes=40 * 2**20),
        cost_estimate=pl.CostEstimate(flops=10**9, bytes_accessed=10**6, transcendentals=0),
    )(view, volume)


_levels = np.exp(3.0 * np.arange(NPTS) / (NPTS - 1)) - 1.0
_levels = _levels / (math.exp(3.0) - 1.0)
_spacing = [float(v) for v in _levels[1:] - _levels[:-1]]
_middle = [float(v) for v in 0.5 * (_levels[1:] + _levels[:-1])]


def face_kernel(tiles, surface, height, kelvin, hot, tile_of, live, h, wall):
    by_slot = surface[...]
    tall = jnp.concatenate([by_slot, jnp.zeros((LANES - 8, LANES), jnp.int32)], axis=0)
    low_bits = jnp.transpose(tall.astype(f32)).astype(jnp.int32) & 127
    lane = lax.broadcasted_iota(jnp.int32, (LANES, LANES), 1)
    for k in range(8):
        hot[pl.ds(k * LANES, LANES), :] = jnp.where(lane == low_bits[:, k : k + 1], 1.0, 0.0).astype(bf16)
    tile_of[...] = jnp.where(by_slot < 0, -1, by_slot >> 7)
    live[...] = jnp.where(lax.broadcasted_iota(jnp.int32, (8, LANES), 0) < tiles[0], 1.0, 0.0)
    h[...] = height[...]
    wall[...] = kelvin[...]


def face_tables(tiles, surface, height, kelvin):
    tile = jax.ShapeDtypeStruct((8, LANES), f32)
    return pl.pallas_call(
        face_kernel,
        out_shape=(
            jax.ShapeDtypeStruct((8 * LANES, LANES), bf16),
            jax.ShapeDtypeStruct((8, LANES), jnp.int32),
            tile,
            tile,
            tile,
        ),
        in_specs=[pl.BlockSpec(memory_space=pltpu.SMEM)]
        + [pl.BlockSpec(memory_space=pltpu.VMEM)] * 3,
        out_specs=(pl.BlockSpec(memory_space=pltpu.VMEM),) * 5,
        compiler_params=pltpu.CompilerParams(vmem_limit_bytes=40 * 2**20),
        cost_estimate=pl.CostEstimate(flops=10**6, bytes_accessed=10**6, transcendentals=0),
    )(tiles, surface, height, kelvin)


def wall_kernel(received, hot, tile_of, alive, height, kelvin, _mark, out):
    table = jnp.transpose(received[...])
    sub = lax.broadcasted_iota(jnp.int32, (8, LANES), 0)
    here = [sub == tile_of[k : k + 1] for k in range(8)]
    spread = jnp.concatenate(
        [
            jnp.concatenate(
                [jnp.where(here[k], table[c * 8 + k : c * 8 + k + 1], 0.0) for k in range(8)], axis=1
            )
            for c in range(5)
        ],
        axis=0,
    )
    parts = jnp.concatenate(split_bf16(spread, 2), axis=0)
    faces = lax.dot_general(parts, hot[...], (((1,), (0,)), ((), ())), preferred_element_type=f32)
    faces = faces[40:] + faces[:40]
    live = alive[...] > 0.5
    filler = (1.0, 0.4, 0.0, 0.0, 3.0)
    rho, mx, my, mz, energy = (
        jnp.where(live, faces[c * 8 : c * 8 + 8], filler[c]) for c in range(5)
    )
    h = height[...]
    wall = kelvin[...]
    power = mx * mx + my * my + mz * mz
    speed = jnp.sqrt(power) / rho
    temperature = 0.4 * (energy - 0.5 * power / rho) / rho
    tau = 0.002 * speed / h

    def inverse(x):
        return pl.reciprocal(x, approx=True)

    def viscosity(tau):
        friction = jnp.sqrt(tau / rho)
        a = rho * 0.41 * friction * h
        b = friction * rho * h * (-math.log2(math.e) / (0.002 * 17.0))
        return a, b

    def eddy(a, b, j):
        damp = 1.0 - jnp.exp2(b * _middle[j])
        return a * (damp * damp)

    def step(_, tau):
        a, b = viscosity(tau)
        total = [jnp.zeros_like(tau) for _ in range(4)]
        for j in range(NPTS - 1):
            total[j % 4] = total[j % 4] + (_spacing[j] / _middle[j]) * inverse(0.002 / _middle[j] + eddy(a, b, j))
        total = (total[0] + total[1]) + (total[2] + total[3])
        return tau * speed / (tau * h * total)

    tau = lax.fori_loop(0, ITERS - 1, step, tau)
    a, b = viscosity(tau)
    total = jnp.zeros_like(tau)
    impedance = jnp.zeros_like(tau)
    work = jnp.zeros_like(tau)
    for j in range(NPTS - 1):
        nu = eddy(a, b, j)
        increment = (_spacing[j] / _middle[j]) * inverse(0.002 / _middle[j] + nu)
        total = total + increment
        part = (_spacing[j] / _middle[j] / (3.5 / 0.9)) * inverse((0.9 / 0.72) * 0.002 / _middle[j] + nu)
        impedance = impedance + part
        work = work + (total - 0.5 * increment) * part
    scale = tau * h
    rate = (temperature - wall + tau * (scale * h * work)) / (h * impedance)
    tau = tau * speed / (scale * total)
    friction = jnp.where(live, 100.0 * tau / (rho * speed * speed), 0.0)
    heat = jnp.where(live, 100.0 * rate / (rho * 3.5 * speed), 0.0)
    for i in range(8):
        out[0:1, i * LANES : (i + 1) * LANES] = friction[i : i + 1]
        out[1:2, i * LANES : (i + 1) * LANES] = heat[i : i + 1]


def wall_faces(received, tables, mark):
    return pl.pallas_call(
        wall_kernel,
        out_shape=jax.ShapeDtypeStruct((2, 8 * LANES), f32),
        in_specs=[pl.BlockSpec(memory_space=pltpu.VMEM)] * 6 + [pl.BlockSpec(memory_space=pl.ANY)],
        out_specs=pl.BlockSpec(memory_space=pltpu.VMEM),
        compiler_params=pltpu.CompilerParams(vmem_limit_bytes=40 * 2**20),
        cost_estimate=pl.CostEstimate(flops=10**8, bytes_accessed=10**6, transcendentals=10**6),
    )(received, *tables, mark)


def pitch_map(across):
    p = lax.broadcasted_iota(jnp.int32, (512, 512), 1 if across else 0)
    n = lax.broadcasted_iota(jnp.int32, (512, 512), 0 if across else 1)
    return jnp.where(p == 4 * (n & 127) + (n >> 7), 1.0, 0.0).astype(bf16)


def put_halves(halves, c, rows):
    hi, low = split_bf16(rows, 2)
    halves[pl.ds(c * 64, 64), :] = hi
    halves[pl.ds(320 + c * 64, 64), :] = low


def remap(halves, table):
    got = lax.dot_general(halves[...], table, (((1,), (0,)), ((), ())), preferred_element_type=f32)
    return got[:320] + got[320:]


def view_kernel(state, view, first, second, halves):
    table = pitch_map(False)
    odd = lax.axis_index("stream") % 2
    row_first = (1 - odd) * (16 - HALO)
    row_second = odd * (16 - HALO)
    for c in range(5):
        put_halves(halves, c, state[c].reshape(64, 512))
    x = remap(halves, table)
    for c in range(5):
        for a in range(4):
            for j in range(QUARTERS):
                at = 64 * c + 16 * a
                view[c, a, j] = x[at : at + 16, j * LANES : (j + 1) * LANES]
    for c in range(5):
        for a in range(4):
            for j in range(QUARTERS):
                at = ((c * 4 + a) * QUARTERS + j) * HALO
                first[pl.ds(at, HALO), :] = view[c, a, j, pl.ds(row_first, HALO), :]
                second[pl.ds(at, HALO), :] = view[c, a, j, pl.ds(row_second, HALO), :]


def view_field(state):
    side = jax.ShapeDtypeStruct((5 * 4 * QUARTERS * HALO, LANES), f32)
    return pl.pallas_call(
        view_kernel,
        out_shape=(jax.ShapeDtypeStruct((5, 4, QUARTERS, 16, LANES), f32), side, side),
        in_specs=[pl.BlockSpec(memory_space=pltpu.VMEM)],
        out_specs=(pl.BlockSpec(memory_space=pltpu.VMEM),) * 3,
        scratch_shapes=[
            pltpu.VMEM((640, 512), bf16),
        ],
        compiler_params=pltpu.CompilerParams(vmem_limit_bytes=40 * 2**20),
        cost_estimate=pl.CostEstimate(flops=10**9, bytes_accessed=3 * 10**6, transcendentals=0),
    )(state)


REACH = ((1, -2, 20, 0), (2, -1, 18, 20), (3, 0, 16, 38))
SIDE = 54


def pack_kernel(view, stream_b, stream_a, _samples, first, second):
    span_odd = lax.axis_index("span") % 2
    stream_odd = lax.axis_index("stream") % 2

    def fill(before, after):
        def body(c, _):
            for out, high in ((first, span_odd == 0), (second, span_odd == 1)):
                for distance, _, count, base in REACH:
                    plane = jnp.where(high, 4 - distance, distance - 1)
                    extra = HALO - distance
                    for j in range(QUARTERS):
                        at = (c * QUARTERS + j) * SIDE + base
                        side = ((c * 4 + plane) * QUARTERS + j) * HALO
                        for i in range(2):
                            out[pl.ds(at + extra + 8 * i, 8), :] = view[c, plane, j, pl.ds(8 * i, 8), :]
                        if extra:
                            out[pl.ds(at, extra), :] = before[pl.ds(side + distance, extra), :]
                            out[pl.ds(at + extra + 16, extra), :] = after[pl.ds(side, extra), :]
            return 0

        lax.fori_loop(0, 5, body, 0)

    @pl.when(stream_odd == 0)
    def _():
        fill(stream_b, stream_a)

    @pl.when(stream_odd == 1)
    def _():
        fill(stream_a, stream_b)


def pack_planes(view, stream_b, stream_a, samples):
    shape = jax.ShapeDtypeStruct((5 * QUARTERS * SIDE, LANES), f32)
    return pl.pallas_call(
        pack_kernel,
        out_shape=(shape, shape),
        in_specs=[pl.BlockSpec(memory_space=pltpu.VMEM)] * 3 + [pl.BlockSpec(memory_space=pl.ANY)],
        out_specs=(pl.BlockSpec(memory_space=pltpu.VMEM),) * 2,
        compiler_params=pltpu.CompilerParams(vmem_limit_bytes=40 * 2**20),
        cost_estimate=pl.CostEstimate(flops=10**6, bytes_accessed=2 * 10**6, transcendentals=0),
    )(view, stream_b, stream_a, samples)


def swap(x, axis, parity):
    spans, streams = lax.axis_size("span"), lax.axis_size("stream")

    def partner(i, n):
        other = i + 1 if i % 2 == parity else i - 1
        return other if 0 <= other < n else None

    pairs = []
    for a in range(spans):
        for b in range(streams):
            if axis == "span":
                other = partner(a, spans)
                there = (a, b ^ 1) if other is None else (other, b)
            else:
                other = partner(b, streams)
                there = (a ^ 1, b) if other is None else (a, other)
            pairs.append((a * streams + b, there[0] * streams + there[1]))
    return lax.ppermute(x, ("span", "stream"), pairs)


NORMAL = ((0, 1, 2, 6), (1, 3, 4, 7), (2, 4, 5, 8))
MIDDLE = (HALO, HALO + 8)


def chunks_from(row):
    return tuple(row - 1 + 8 * i for i in range(3))


def primitive(u):
    rho, m1, m2, m3, energy = u
    inv = pl.reciprocal(rho, approx=True)

    v1, v2, v3 = m1 * inv, m2 * inv, m3 * inv
    t11, t22, t33 = m1 * v1, m2 * v2, m3 * v3
    pressure = 0.4 * energy - 0.2 * (t11 + t22 + t33)
    total = energy + pressure
    square = 1.4 * pressure * inv
    sound = square * lax.rsqrt(square) + 0.04
    return [
        t11 + pressure,
        m1 * v2,
        m1 * v3,
        t22 + pressure,
        m2 * v3,
        t33 + pressure,
        total * v1,
        total * v2,
        total * v3,
        jnp.abs(v1) + sound,
        jnp.abs(v2) + sound,
        jnp.abs(v3) + sound,
    ]


def after(x):
    return jnp.concatenate([x[1:], pltpu.roll(x[:1], LANES - 1, 2)], axis=0)


def before(x):
    return jnp.concatenate([pltpu.roll(x[-1:], 1, 2), x[:-1]], axis=0)


def stage_tools(src, der, gspan, gstream, finish):
    def fill(p, rows):
        for r in rows:
            at = pl.ds(r, 8)
            for n, d in enumerate(primitive([src[c, p, :, at, :] for c in range(5)])):
                der[n, p, :, at, :] = d

    def flux(c, k, p, at):
        return src[1 + k, p, :, at, :] if c == 0 else der[NORMAL[k][c - 1], p, :, at, :]

    def span_faces(p, rows, slot):
        for r in rows:
            at = pl.ds(r, 8)
            coef = jnp.maximum(der[9, p, :, at, :], der[9, p + 1, :, at, :])
            for c in range(5):
                g = (coef - 0.04 if c == 0 else coef) * (src[c, p + 1, :, at, :] - src[c, p, :, at, :])
                gspan[slot, c, :, at, :] = g - (flux(c, 0, p, at) + flux(c, 0, p + 1, at))

    def outputs(p, rows, whole, low_slot, high_slot, faces):
        for i, r in enumerate(rows):
            at, up, down = pl.ds(r, 8), pl.ds(r + 1, 8), pl.ds(r - 1, 8)
            here = der[11, p, :, at, :]
            stream_wave = der[10, p, :, at, :]
            coef_stream = jnp.maximum(stream_wave, der[10, p, :, up, :])
            coef_pitch = jnp.maximum(here, after(here))
            direct = whole and i == 0
            if direct:
                coef_down = jnp.maximum(stream_wave, der[10, p, :, down, :])
            if faces:
                coef_span = jnp.maximum(der[9, p, :, at, :], der[9, p + 1, :, at, :])
            for c in range(5):

                def weigh(coef):
                    return coef - 0.04 if c == 0 else coef

                u = src[c, p, :, at, :]
                if faces:
                    g = weigh(coef_span) * (src[c, p + 1, :, at, :] - u)
                    g = g - (flux(c, 0, p, at) + flux(c, 0, p + 1, at))
                    gspan[high_slot, c, :, at, :] = g
                else:
                    g = gspan[high_slot, c, :, at, :]
                acc = g - gspan[low_slot, c, :, at, :]
                f = flux(c, 1, p, at)
                g = weigh(coef_stream) * (src[c, p, :, up, :] - u) - (f + flux(c, 1, p, up))
                gstream[c, :, pl.ds(r + 8, 8), :] = g
                if direct:
                    low = weigh(coef_down) * (u - src[c, p, :, down, :]) - (f + flux(c, 1, p, down))
                else:
                    low = gstream[c, :, pl.ds(r + 7, 8), :]
                acc = acc + (g - low)
                f = flux(c, 2, p, at)
                h = weigh(coef_pitch) * (after(u) - u) - (f + after(f))
                finish(c, p, r, i, u, acc + (h - before(h)))

    return fill, span_faces, outputs


def clamp_planes(e):
    at = lax.axis_index("span")

    def copy(dst, src):
        for c in range(5):
            for i in range(3):
                e[c, dst, :, pl.ds(8 * i, 8), :] = e[c, src, :, pl.ds(8 * i, 8), :]

    @pl.when(at == 0)
    def _():
        copy(2, 3)

    @pl.when(at == lax.axis_size("span") - 1)
    def _():
        copy(7, 6)


def clamp_rows(e, planes):
    at = lax.axis_index("stream")

    def copy(dst, src):
        for c in range(5):
            for p in planes:
                for q in range(QUARTERS):
                    e[c, p, q, pl.ds(dst, 1), :] = e[c, p, q, pl.ds(src, 1), :]

    @pl.when(at == 0)
    def _():
        copy(2, 3)

    @pl.when(at == lax.axis_size("stream") - 1)
    def _():
        copy(19, 18)


def first_stage(e0, e1):
    def finish(c, p, r, i, u, acc):
        e1[c, p, :, pl.ds(r, 8), :] = u + 0.05 * acc

    return finish


def inner_kernel(view, stream_a, stream_b, e0, e1, der, table, gspan, gstream):
    odd = lax.axis_index("stream") % 2

    def own(c, _):
        for p in range(4):
            for i in range(2):
                e0[c, HALO + p, :, pl.ds(HALO + 8 * i, 8), :] = view[c, p, :, pl.ds(8 * i, 8), :]
        return 0

    lax.fori_loop(0, 5, own, 0)

    def halo_rows(before, after):
        def body(c, _):
            for p in range(4):
                for j in range(QUARTERS):
                    at = ((c * 4 + p) * QUARTERS + j) * HALO
                    e0[c, HALO + p, j, pl.ds(0, HALO), :] = before[pl.ds(at, HALO), :]
                    e0[c, HALO + p, j, pl.ds(HALO + 16, HALO), :] = after[pl.ds(at, HALO), :]
            return 0

        lax.fori_loop(0, 5, body, 0)

    @pl.when(odd == 0)
    def _():
        halo_rows(stream_b, stream_a)

    @pl.when(odd == 1)
    def _():
        halo_rows(stream_a, stream_b)

    clamp_rows(e0, range(3, 7))
    fill, span_faces, outputs = stage_tools(e0, der, gspan, gstream, first_stage(e0, e1))
    wide = chunks_from(1)

    def prims(p, _):
        fill(p, wide)
        return 0

    lax.fori_loop(3, 7, prims, 0)
    span_faces(3, wide, 1)

    def plane(p, _):
        outputs(p, wide, False, 1 - (p & 1), p & 1, True)
        return 0

    lax.fori_loop(4, 6, plane, 0)
    table[...] = pitch_map(True)


def inner_planes(view, stream_a, stream_b):
    block = jax.ShapeDtypeStruct((5, 10, QUARTERS, ROWS, LANES), f32)
    return pl.pallas_call(
        inner_kernel,
        out_shape=(
            block,
            block,
            jax.ShapeDtypeStruct((12, 10, QUARTERS, ROWS, LANES), f32),
            jax.ShapeDtypeStruct((512, 512), bf16),
        ),
        in_specs=[pl.BlockSpec(memory_space=pltpu.VMEM)] * 3,
        out_specs=(pl.BlockSpec(memory_space=pltpu.VMEM),) * 4,
        scratch_shapes=[
            pltpu.VMEM((3, 5, QUARTERS, ROWS, LANES), f32),
            pltpu.VMEM((5, QUARTERS, ROWS + 8, LANES), f32),
        ],
        compiler_params=pltpu.CompilerParams(vmem_limit_bytes=LIMIT_INNER),
        cost_estimate=pl.CostEstimate(flops=10, bytes_accessed=10, transcendentals=0),
    )(view, stream_a, stream_b)


def field_kernel(
    span_a, span_b, table, _e0, _e1, _der, _tile_of, out, mark, e0, e1, der, e2, gspan, gstream, done, result, sems
):
    odd = lax.axis_index("span") % 2

    def halo_planes(before, after):
        def body(c, _):
            for src, high in ((before, False), (after, True)):
                for distance, row, count, base in REACH:
                    plane = 6 + distance if high else HALO - distance
                    for j in range(QUARTERS):
                        at = (c * QUARTERS + j) * SIDE + base
                        for i in range(0, count, 8):
                            n = min(8, count - i)
                            e0[c, plane, j, pl.ds(HALO + row + i, n), :] = src[pl.ds(at + i, n), :]
            return 0

        lax.fori_loop(0, 5, body, 0)

    @pl.when(odd == 0)
    def _():
        halo_planes(span_b, span_a)

    @pl.when(odd == 1)
    def _():
        halo_planes(span_a, span_b)

    clamp_planes(e0)
    clamp_rows(e0, (1, 2, 7, 8))

    fill, span_faces, outputs = stage_tools(e0, der, gspan, gstream, first_stage(e0, e1))
    wide = chunks_from(1)
    fill(0, MIDDLE)
    fill(9, MIDDLE)

    def prims(i, _):
        fill(jnp.where(i < 2, 1 + i, 5 + i), wide)
        return 0

    lax.fori_loop(0, 4, prims, 0)
    span_faces(0, MIDDLE, 0)
    span_faces(1, wide, 1)
    outputs(1, MIDDLE, True, 0, 1, False)
    span_faces(5, wide, 2)

    def plane_one(i, _):
        p = jnp.where(i < 2, 2 + i, 4 + i)
        high = i & 1
        outputs(p, wide, False, jnp.where(i == 2, 2, 1 - high), high, True)
        return 0

    lax.fori_loop(0, 4, plane_one, 0)
    outputs(8, MIDDLE, True, 1, 0, True)

    def finish_two(c, p, r, i, u, acc):
        e2[c, p, :, pl.ds(r, 8), :] = 3.0 * e0[c, p, :, pl.ds(r, 8), :] + (u + 0.05 * acc)

    clamp_planes(e1)
    clamp_rows(e1, range(2, 8))
    fill, span_faces, outputs = stage_tools(e1, der, gspan, gstream, finish_two)
    wide_two = chunks_from(2)
    fill(1, MIDDLE)
    fill(2, wide_two)
    span_faces(1, MIDDLE, 1)
    fill(3, wide_two)
    span_faces(2, wide_two, 0)
    outputs(2, MIDDLE, True, 1, 0, False)

    def plane_two(p, _):
        fill(p + 1, wide_two)
        outputs(p, wide_two, False, 1 - (p & 1), p & 1, True)
        return 0

    lax.fori_loop(3, 7, plane_two, 0)
    fill(8, MIDDLE)
    outputs(7, MIDDLE, True, 0, 1, True)

    def finish_three(c, p, r, i, u, acc):
        new = (1.0 / 3.0) * e0[c, p, :, pl.ds(r, 8), :] + ((0.5 / 3.0) * u + (0.025 / 3.0) * acc)
        for q in range(QUARTERS):
            done[p - HALO, pl.ds(16 * c + 8 * i, 8), q * LANES : (q + 1) * LANES] = new[q]

    copies = []

    def write(p):
        hi, low = split_bf16(done[p], 2)
        got = lax.dot_general(
            jnp.concatenate([hi, low], axis=0),
            table[...],
            (((1,), (0,)), ((), ())),
            preferred_element_type=f32,
        )
        result[p] = (got[:80] + got[80:]).reshape(5, 16, 512)
        copies.append(pltpu.make_async_copy(result.at[p], out.at[:, p], sems.at[p]))
        copies[-1].start()

    clamp_planes(e2)
    clamp_rows(e2, range(3, 7))
    fill, span_faces, outputs = stage_tools(e2, der, gspan, gstream, finish_three)
    wide_three = chunks_from(3)
    fill(2, MIDDLE)
    fill(3, wide_three)
    span_faces(2, MIDDLE, 0)
    for p in range(3, 7):
        fill(p + 1, wide_three if p < 6 else MIDDLE)
        outputs(p, MIDDLE, True, 1 - (p & 1), p & 1, True)
        if p > 3:
            write(p - HALO - 1)
    write(3)
    mark[...] = jnp.zeros((8, LANES), f32)
    for copy in copies:
        copy.wait()


def advance_field(span_a, span_b, inner, tile_of):
    e0, e1, der, table = inner
    vmem = pl.BlockSpec(memory_space=pltpu.VMEM)
    anywhere = pl.BlockSpec(memory_space=pl.ANY)
    out = pl.pallas_call(
        field_kernel,
        out_shape=(
            jax.ShapeDtypeStruct((5, 4, 16, 512), f32),
            jax.ShapeDtypeStruct((8, LANES), f32),
            jax.ShapeDtypeStruct(e0.shape, f32),
            jax.ShapeDtypeStruct(e1.shape, f32),
            jax.ShapeDtypeStruct(der.shape, f32),
        ),
        in_specs=[vmem] * 6 + [anywhere],
        out_specs=(anywhere,) + (vmem,) * 4,
        input_output_aliases={3: 2, 4: 3, 5: 4},
        scratch_shapes=[
            pltpu.VMEM((5, 10, QUARTERS, ROWS, LANES), f32),
            pltpu.VMEM((3, 5, QUARTERS, ROWS, LANES), f32),
            pltpu.VMEM((5, QUARTERS, ROWS + 8, LANES), f32),
            pltpu.VMEM((4, 80, 512), f32),
            pltpu.VMEM((4, 5, 16, 512), f32),
            pltpu.SemaphoreType.DMA((4,)),
        ],
        compiler_params=pltpu.CompilerParams(vmem_limit_bytes=LIMIT_FIELD),
        cost_estimate=pl.CostEstimate(flops=10, bytes_accessed=10, transcendentals=0),
    )(span_a, span_b, table, e0, e1, der, tile_of)
    return out[0], out[1]


def per_device(state, tiles, volume, surface, height, kelvin):
    view, first, second = view_field(state)
    stream_a, stream_b = swap(first, "stream", 0), swap(second, "stream", 1)

    outgoing = gather_samples(view, volume[0].T)
    received = lax.all_to_all(outgoing, ("span", "stream"), 0, 0, tiled=True)

    first, second = pack_planes(view, stream_b, stream_a, outgoing)
    span_a, span_b = swap(first, "span", 0), swap(second, "span", 1)
    tables = face_tables(tiles, surface[0].T, height.reshape(8, LANES), kelvin.reshape(8, LANES))
    inner = inner_planes(view, stream_a, stream_b)
    field, mark = advance_field(span_a, span_b, inner, tables[1])
    return field, wall_faces(received, tables, mark)


def solution(mesh):
    in_specs = (
        P(None, "span", "stream", None),
        P(("span", "stream")),
        P(("span", "stream"), None, None),
        P(("span", "stream"), None, None),
        P(("span", "stream")),
        P(("span", "stream")),
    )
    out_specs = (P(None, "span", "stream", None), P(None, ("span", "stream")))
    return jax.shard_map(per_device, mesh=mesh, in_specs=in_specs, out_specs=out_specs, check_vma=False)
```
